32 devices in a mesh: seq: 4 (over z), tensor: 8 (over y, x, core).
Axes of the slice: x: 2, y: 2, z: 4, core: 2. Of those that a mesh axis runs over, the one named last changes fastest.
Arguments:
- layer_inputs: bfloat16 [768, 6144], P('seq'), may hold values from -16 to 16
- projection_matrices: bfloat16 [6144, 3, 768], P(None, None, 'tensor'), may hold values from -0.109375 to 0.109375
- result_sensitivity: bfloat16 [768, 768], P('seq', 'tensor'), may hold values from -4.5 to 4.5
- channel_fading_rate: float32 [8], P('tensor'), may hold values from 2.6041667e-05 to 0.03
- loss_events: int32 [4], replicated, may hold values from 0 to 767
Outputs:
- input_grad: bfloat16 [6144, 768], P('tensor', 'seq')
- weight_grad: bfloat16 [6144, 3, 768], P('seq', None, 'tensor')
The draws below stay inside these ranges and needn't reach their ends.
All inputs are finite; a program needn't handle non-finite values.
Results may differ from the reference program's by a relative error of at most 0.023.
Values may be sent and summed in bfloat16 or wider, within the bound.
A program may use at most 64 MiB of HBM per device.

```python
import math
import jax
import jax.numpy as jnp
from jax import lax

D = 6144
DH = 96
TOK_DEV = 192
MEMORY_LOSSES = 4
HEADS = 8
SEQUENCE_LENGTH = 768
N_SEQ = 4


SPIKE_FACTOR = 4.0


INPUT_LIMIT = 16.0


SENSITIVITY_LIMIT = 4.5


def draw_channel_fading_rate(key, part):
    lower = math.log(0.02 / SEQUENCE_LENGTH)
    upper = math.log(0.03)
    spread = jax.random.uniform(key, (HEADS,), jnp.float32, lower, upper)
    return jnp.exp(spread)


def draw_layer_inputs(key, part):
    noise_key = jax.random.fold_in(key, 11)
    common_key = jax.random.fold_in(key, 12)
    pair_key = jax.random.fold_in(key, 13)
    rows = jnp.arange(SEQUENCE_LENGTH, dtype=jnp.int32)
    shard = rows // TOK_DEV
    signs = 1.0 - 2.0 * (shard % 2).astype(jnp.float32)
    common = jax.random.normal(common_key, (D,), jnp.float32)
    noise = jax.random.normal(noise_key, (SEQUENCE_LENGTH, D), jnp.float32)
    base = signs[:, None] * common[None, :] + noise
    pairing = jax.random.permutation(pair_key, N_SEQ).astype(jnp.int32)
    column_block = jnp.arange(D, dtype=jnp.int32) // (D // N_SEQ)
    paired = pairing[shard]
    marked = paired[:, None] == column_block[None, :]
    values = jnp.where(marked, SPIKE_FACTOR * base, base)
    return jnp.clip(values, -INPUT_LIMIT, INPUT_LIMIT).astype(jnp.bfloat16)


def draw_result_sensitivity(key, part):
    noise_key = jax.random.fold_in(key, 21)
    common_key = jax.random.fold_in(key, 22)
    common = jax.random.normal(common_key, (HEADS * DH,), jnp.float32)
    noise = jax.random.normal(noise_key, (SEQUENCE_LENGTH, HEADS * DH), jnp.float32)
    values = common[None, :] + noise
    return jnp.clip(values, -SENSITIVITY_LIMIT, SENSITIVITY_LIMIT).astype(jnp.bfloat16)


def plant(drawn, stream_key, low, largest):
    index_at = [jax.random.randint(jax.random.fold_in(stream_key, axis), (), 0, length) for axis, length in enumerate(drawn.shape)]
    longest = drawn.shape.index(max(drawn.shape))
    next_to = index_at[:longest] + [(index_at[longest] + 1) % drawn.shape[longest]] + index_at[longest + 1:]
    return drawn.at[tuple(index_at)].set(low).at[tuple(next_to)].set(largest)


def with_spikes(entries, stream_key, source, target, shards_of, factor):
    def block_of(position):
        return (jnp.arange(entries.shape[position]) // (entries.shape[position] // shards_of)).reshape((-1,) + (1,) * (entries.ndim - 1 - position))

    near = jax.random.permutation(stream_key, shards_of)[block_of(target)]
    other_side = (block_of(target) + shards_of // 2) % shards_of
    return jnp.where((block_of(source) == near) | (block_of(source) == other_side), factor * entries, entries)


def shard_levels(stream_key, shape, pieces, least, top_value):
    level, own = 1.0, jax.random.fold_in(stream_key, 6)
    for dim, parts in pieces:
        steps = jnp.exp(jax.random.uniform(jax.random.fold_in(own, dim), (parts,), jnp.float32, least / len(pieces), top_value / len(pieces)))
        level = level * jnp.repeat(steps, shape[dim] // parts).reshape([-1 if axis == dim else 1 for axis in range(len(shape))])
    return level


def heavy_noise(own_key, dims, scale, most, pieces, heavy, kind=jnp.bfloat16):
    values = scale * jax.random.normal(own_key, dims, jnp.float32)
    if pieces:
        values = values * shard_levels(own_key, dims, pieces, -0.22, 0.18)
    return jnp.clip(with_spikes(values, jax.random.fold_in(own_key, 3), *heavy), -most, most).astype(kind)


def setup_inputs(seed: int = 0) -> dict:
    key_of = jax.random.split(jax.random.key(seed), 6)
    return {
        "layer_inputs": draw_layer_inputs(jax.random.fold_in(key_of[5], 71), 0),
        "projection_matrices": heavy_noise(key_of[1], (D, 3, HEADS * DH), D ** -0.5, 0.109375, ((2, 8),), (2, 0, 8, 2.0)),
        "result_sensitivity": draw_result_sensitivity(jax.random.fold_in(key_of[5], 71), 0),
        "channel_fading_rate": draw_channel_fading_rate(jax.random.fold_in(key_of[5], 71), 0),
        "loss_events": plant(jax.random.randint(key_of[4], (MEMORY_LOSSES,), 0, SEQUENCE_LENGTH), jax.random.fold_in(key_of[4], 1), 0, SEQUENCE_LENGTH - 1).astype(jnp.int32),
    }


DROP_LOGARITHM = 0.3
CLIP_RMS = 0.5

def head_grads(operands):
    query, keys, values, grads_out, logarithm_values = operands
    cumul = jnp.cumsum(logarithm_values)
    length = query.shape[0]
    later = jnp.arange(length)[:, None] >= jnp.arange(length)[None, :]
    weight = jnp.exp(jnp.where(later, cumul[:, None] - cumul[None, :], -jnp.inf))
    highest = lax.Precision.HIGHEST
    scores = jnp.dot(query, keys.T, precision=highest) * weight
    dscores = jnp.dot(grads_out, values.T, precision=highest) * weight
    dquery = jnp.dot(dscores, keys, precision=highest)
    dkey = jnp.dot(dscores.T, query, precision=highest)
    dvalue = jnp.dot(scores.T, grads_out, precision=highest)
    return (dquery, dkey, dvalue)

def reference(layer_inputs, projection_matrices, result_sensitivity, channel_fading_rate, loss_events):
    scale = DH ** (-0.5)
    width = HEADS * DH
    flat_w = projection_matrices.reshape(D, 3 * width)
    proj = jnp.dot(layer_inputs, flat_w, preferred_element_type=jnp.float32).reshape(SEQUENCE_LENGTH, 3, HEADS, DH)
    query = (proj[:, 0] * scale).astype(jnp.bfloat16).astype(jnp.float32).transpose(1, 0, 2)
    keys = proj[:, 1].astype(jnp.bfloat16).astype(jnp.float32).transpose(1, 0, 2)
    values = proj[:, 2].astype(jnp.bfloat16).astype(jnp.float32).transpose(1, 0, 2)
    grads_out = result_sensitivity.reshape(SEQUENCE_LENGTH, HEADS, DH).astype(jnp.float32).transpose(1, 0, 2)
    element_location = jnp.arange(SEQUENCE_LENGTH, dtype=jnp.int32)
    memory_loss_sites = lax.optimization_barrier(jnp.sum((loss_events[None, :] == element_location[:, None]).astype(jnp.float32), axis=1))
    logarithm_values = -(channel_fading_rate[:, None] + DROP_LOGARITHM * memory_loss_sites[None, :])
    dquery, dkey, dvalue = lax.map(head_grads, (query, keys, values, grads_out, logarithm_values))
    stacked = jnp.stack([dquery * scale, dkey, dvalue]).astype(jnp.bfloat16)
    gflat = stacked.transpose(2, 0, 1, 3).reshape(SEQUENCE_LENGTH, 3 * width)
    input_grad = jnp.dot(flat_w, gflat.T, preferred_element_type=jnp.float32).astype(jnp.bfloat16)
    token_blocks = layer_inputs.reshape(N_SEQ, TOK_DEV, D)
    grad_blocks = gflat.reshape(N_SEQ, TOK_DEV, 3 * width)

    def add_block(total, pair):
        block_term = jnp.dot(pair[0].T, pair[1], preferred_element_type=jnp.float32)
        rounded = lax.optimization_barrier(block_term.astype(jnp.bfloat16))
        return (total + rounded.astype(jnp.float32), None)
    summed, _ = lax.scan(add_block, jnp.zeros((D, 3 * width), jnp.float32), (token_blocks, grad_blocks))
    square = jnp.sum(summed * summed)
    factor = jnp.minimum(1.0, CLIP_RMS * math.sqrt(D * 3 * width) / jnp.sqrt(square + 1e-06))
    weight_grad = (summed * factor).astype(jnp.bfloat16).reshape(D, 3, width)
    return (input_grad, weight_grad)
```

```python
import functools
import math

import jax
import jax.numpy as jnp
from jax import lax
from jax.experimental import pallas as pl
from jax.experimental.pallas import tpu as pltpu
from jax.sharding import PartitionSpec as P

DH = 96
DROP_LOGARITHM = 0.3
CLIP_RMS = 0.5
MESH = pl.DeviceIdType.MESH
F32 = jnp.float32
BF16 = jnp.bfloat16
LOAD_CHUNKS = 4


def mm(a, b):
    return jnp.dot(a, b, preferred_element_type=F32)


def mm_nt(a, b):
    return lax.dot_general(a, b, (((1,), (1,)), ((), ())), preferred_element_type=F32)


def kernel(
    n_seq, n_t, entries, aligned,
    x_hbm, w_hbm, wb_hbm, o_ref, rate_ref, events_ref,
    ig_ref, wg_ref,
    x, w, wb, xg, g, gt, st, ps, rc, sd, rd, acc, sqz, sqt,
    load_sem, bx1s, bx1r, bx2s, bx2r, bx3s, bx3r, sts, str_, gs, gr,
    pss, psr, rds, rdr, zs, zr, ts, tr,
):
    rows, width = x_hbm.shape
    blk = width // n_seq
    iblk = width // n_t
    scale = DH ** (-0.5)
    s = lax.axis_index("seq")
    j = lax.axis_index("tensor")
    nc = n_t // 2
    k = lax.rem(j, 2)
    chip = j // 2
    sibling = j + 1 - 2 * k
    group = (j // 8) * 8
    c = lax.rem(j, 8) // 2
    q = blk // 4
    half = rows // 2

    wide = width // LOAD_CHUNKS
    loads = []
    for i in range(LOAD_CHUNKS):
        cols = pl.ds(i * wide, wide)
        for n, (src, dst) in enumerate(((x_hbm, x), (w_hbm, w))):
            copy = pltpu.make_async_copy(src.at[:, cols], dst.at[:, cols], load_sem.at[2 * i + n])
            copy.start()
            loads.append(copy)
    if not aligned:
        wb_copy = pltpu.make_async_copy(wb_hbm, wb, load_sem.at[2 * LOAD_CHUNKS])
        wb_copy.start()

    def seq_peer(d):
        return lax.rem(s + d, n_seq)

    def t_peer(d):
        return lax.rem(j + d, n_t)

    barrier = pltpu.get_barrier_semaphore()
    for d in range(1, n_seq):
        pl.semaphore_signal(barrier, inc=1, device_id=(seq_peer(d), j), device_id_type=MESH)
    for d in range(1, n_t):
        pl.semaphore_signal(barrier, inc=1, device_id=(s, t_peer(d)), device_id_type=MESH)
    pl.semaphore_wait(barrier, n_seq + n_t - 2)

    sends = []

    def send(src, dst, ssem, rsem, device):
        copy = pltpu.make_async_remote_copy(
            src_ref=src, dst_ref=dst, send_sem=ssem, recv_sem=rsem,
            device_id=device, device_id_type=MESH,
        )
        copy.start()
        sends.append(copy)

    def wait_recv(ref, ssem, rsem, device):
        pltpu.make_async_remote_copy(
            src_ref=ref, dst_ref=ref, send_sem=ssem, recv_sem=rsem,
            device_id=device, device_id_type=MESH,
        ).wait_recv()

    def piece(d, core, chip_col):
        return xg.at[
            d - 1,
            pl.ds(pl.multiple_of(core * half, 32), half),
            pl.ds(pl.multiple_of(chip_col * q, 128), q),
        ]

    def token_half(d, core):
        return xg.at[d - 1, pl.ds(pl.multiple_of(core * half, 32), half), :]

    for d in range(1, n_seq):
        src = x_hbm.at[
            pl.ds(pl.multiple_of(k * half, 32), half),
            pl.ds(pl.multiple_of(seq_peer(d) * blk + c * q, 128), q),
        ]
        send(src, piece(d, k, c), bx1s.at[d - 1], bx1r.at[d - 1], (seq_peer(d), j))

    proj = jnp.zeros((3 * DH, rows), F32)
    for i in range(LOAD_CHUNKS):
        cols = pl.ds(i * wide, wide)
        loads[2 * i].wait()
        loads[2 * i + 1].wait()
        proj = proj + mm_nt(w[:, cols], x[:, cols])
    q_t = (proj[:DH] * scale).astype(BF16)
    k_t = proj[DH : 2 * DH].astype(BF16)
    v_t = proj[2 * DH :].astype(BF16)
    o = o_ref[...]
    o_t = o.astype(F32).T.astype(BF16)
    q_r = q_t.astype(F32).T.astype(BF16)
    v_r = v_t.astype(F32).T.astype(BF16)

    rate = rate_ref[0]
    n_events = events_ref.shape[0]
    base = s * rows
    lane = lax.broadcasted_iota(jnp.int32, (1, rows), 1)

    def events_in(low, high):
        total = jnp.zeros(jnp.broadcast_shapes(jnp.shape(low), jnp.shape(high)), F32)
        for n in range(n_events):
            e = events_ref[n]
            total = total + jnp.where((e > low) & (e <= high), 1.0, 0.0)
        return total

    last = jnp.full((1, rows), rows - 1, jnp.int32) + base
    before = jnp.full((1, rows), -1, jnp.int32) + base
    here = lane + base
    head_w = jnp.exp(-(rate * (lane + 1).astype(F32) + DROP_LOGARITHM * events_in(before, here)))
    tail_w = jnp.exp(
        -(rate * (rows - 1 - lane).astype(F32) + DROP_LOGARITHM * events_in(here, last))
    )

    st[0, 0] = mm((k_t.astype(F32) * tail_w).astype(BF16), v_r).astype(BF16)
    st[1, 0] = mm((q_t.astype(F32) * head_w).astype(BF16), o).astype(BF16)
    for d in range(1, n_seq):
        earlier = jnp.where(seq_peer(d) < s, 1, 0)
        send(st.at[earlier, 0], st.at[0, d], sts.at[d - 1], str_.at[d - 1], (seq_peer(d), j))

    for d in range(1, n_seq):
        wait_recv(piece(d, k, c), bx1s.at[d - 1], bx1r.at[d - 1], (s, j))
        for m in range(1, 4):
            to = group + 2 * lax.rem(c + m, 4) + k
            mine = piece(d, k, c)
            send(mine, mine, bx2s.at[d - 1, m - 1], bx2r.at[d - 1, m - 1], (s, to))

    t_idx = lax.broadcasted_iota(jnp.int32, (rows, rows), 0)
    s_idx = lax.broadcasted_iota(jnp.int32, (rows, rows), 1)
    decay = rate * (t_idx - s_idx).astype(F32) + DROP_LOGARITHM * events_in(
        s_idx + base, t_idx + base
    )
    weight = jnp.where(t_idx >= s_idx, jnp.exp(-jnp.maximum(decay, 0.0)), 0.0)
    scores = (mm(q_r, k_t) * weight).astype(BF16)
    dscores = (mm(o, v_t) * weight).astype(BF16)
    dq_t = mm_nt(k_t, dscores)
    dk_t = mm(q_t, dscores)
    dv_t = mm(o_t, scores)

    prefix = jnp.zeros((DH, DH), F32)
    suffix = jnp.zeros((DH, DH), F32)
    zero = jnp.zeros((1, DH), jnp.int32)
    for d in range(1, n_seq):
        wait_recv(st.at[0, d], sts.at[d - 1], str_.at[d - 1], (s, j))
        src = lax.rem(s + n_seq - d, n_seq)
        state = st[0, d].astype(F32)
        low = jnp.minimum(src, s)
        high = jnp.maximum(src, s)
        gap = rate * ((high - low - 1) * rows).astype(F32) + DROP_LOGARITHM * events_in(
            zero + ((low + 1) * rows - 1), zero + (high * rows - 1)
        )
        state = state * jnp.exp(-gap)
        is_fwd = (zero + src) < (zero + s)
        prefix = prefix + jnp.where(is_fwd, state, 0.0)
        suffix = suffix + jnp.where(is_fwd, 0.0, state)
    dq_t = dq_t + mm(prefix.astype(BF16), o_t) * head_w
    dk_t = dk_t + mm(suffix.astype(BF16), v_t) * tail_w
    dv_t = dv_t + mm(suffix.T.astype(BF16), k_t) * tail_w
    grads_t = jnp.concatenate([dq_t * scale, dk_t, dv_t], axis=0)
    gt[0] = grads_t.astype(BF16)
    g[...] = grads_t.T.astype(BF16)
    for d in range(1, n_seq):
        send(gt.at[0], gt.at[d], gs.at[d - 1], gr.at[d - 1], (seq_peer(d), j))

    step = 256 if iblk % 256 == 0 else iblk
    if not aligned:
        wb_copy.wait()

    def block_term(owner, put):
        if aligned:
            def one(i, carry):
                cols = pl.ds(pl.multiple_of(owner * iblk + i * step, 128), step)
                put(pl.ds(pl.multiple_of(i * step, 128), step), mm(g[...], w[:, cols]))
                return carry
            lax.fori_loop(0, iblk // step, one, 0)
        else:
            put(pl.ds(0, iblk), mm(g[...], wb[owner]))

    for m in range(1, nc + 1):
        to_chip = lax.rem(chip + m, nc)
        def put(cols, value, m=m):
            ps[m - 1, :, cols] = value.astype(BF16)
        block_term(2 * to_chip + 1 - k, put)
        send(ps.at[m - 1], rc.at[m - 1], pss.at[m - 1], psr.at[m - 1], (s, sibling))

    for d in range(1, n_seq):
        for m in range(1, 4):
            wait_recv(
                piece(d, k, lax.rem(c + 4 - m, 4)),
                bx2s.at[d - 1, m - 1], bx2r.at[d - 1, m - 1], (s, j),
            )
        send(token_half(d, k), token_half(d, k), bx3s.at[d - 1], bx3r.at[d - 1], (s, sibling))

    for m in range(1, nc):
        wait_recv(rc.at[m - 1], pss.at[m - 1], psr.at[m - 1], (s, sibling))
        to_chip = lax.rem(chip + m, nc)
        def put(cols, value, m=m):
            sd[m - 1, :, cols] = (value + rc[m - 1, :, cols].astype(F32)).astype(BF16)
        block_term(2 * to_chip + k, put)
        send(sd.at[m - 1], rd.at[m - 1], rds.at[m - 1], rdr.at[m - 1], (s, 2 * to_chip + k))

    wstep = 256
    for d in range(1, n_seq):
        wait_recv(token_half(d, 1 - k), bx3s.at[d - 1], bx3r.at[d - 1], (s, sibling))
        wait_recv(gt.at[d], gs.at[d - 1], gr.at[d - 1], (s, j))

    def grad_cols(i, square):
        cols = pl.ds(pl.multiple_of(i * wstep, 128), wstep)
        total = mm(gt[0], x[:, pl.ds(pl.multiple_of(s * blk + i * wstep, 128), wstep)])
        for d in range(1, n_seq):
            total = total + mm(gt[d], xg[d - 1, :, cols])
        acc[:, cols] = total
        return square + jnp.sum((total * total).reshape(3 * DH // 8, 8, wstep), axis=0)

    square = lax.fori_loop(0, blk // wstep, grad_cols, jnp.zeros((8, wstep), F32))
    sqz[0] = square[:, :128] + square[:, 128:]
    for d in range(1, n_seq):
        send(sqz.at[0], sqz.at[d], zs.at[d - 1], zr.at[d - 1], (seq_peer(d), j))

    wait_recv(rc.at[nc - 1], pss.at[nc - 1], psr.at[nc - 1], (s, sibling))
    for m in range(1, nc):
        wait_recv(rd.at[m - 1], rds.at[m - 1], rdr.at[m - 1], (s, j))

    def put(cols, value):
        total = value + rc[nc - 1, :, cols].astype(F32)
        for m in range(1, nc):
            total = total + rd[m - 1, :, cols].astype(F32)
        ig_ref[:, cols] = total.astype(BF16)

    for d in range(1, n_seq):
        wait_recv(sqz.at[d], zs.at[d - 1], zr.at[d - 1], (s, j))
    total = sqz[0]
    for d in range(1, n_seq):
        total = total + sqz[d]
    sqt[0] = total
    for d in range(1, n_t):
        send(sqt.at[0], sqt.at[d], ts.at[d - 1], tr.at[d - 1], (s, t_peer(d)))
    block_term(j, put)
    for d in range(1, n_t):
        wait_recv(sqt.at[d], ts.at[d - 1], tr.at[d - 1], (s, j))
    total = sqt[0]
    for d in range(1, n_t):
        total = total + sqt[d]
    total = jnp.sum(jnp.sum(total, axis=1, keepdims=True), axis=0, keepdims=True)
    factor = jnp.minimum(1.0, CLIP_RMS * math.sqrt(entries) / jnp.sqrt(total + 1e-06))

    def scaled(i, carry):
        cols = pl.ds(pl.multiple_of(i * wstep, 128), wstep)
        wg_ref[:, cols] = (acc[:, cols] * factor).astype(BF16)
        return carry

    lax.fori_loop(0, blk // wstep, scaled, 0)
    for copy in sends:
        copy.wait_send()


def body(n_seq, n_t, layer_inputs, projection_matrices, result_sensitivity, rate, events):
    rows, width = layer_inputs.shape
    blk, iblk, nc = width // n_seq, width // n_t, n_t // 2
    aligned = iblk % 128 == 0
    w_t = projection_matrices.transpose(1, 2, 0).reshape(3 * DH, width)
    if aligned:
        w_b = jnp.zeros((1, 8, 128), BF16)
    else:
        w_b = w_t.reshape(3 * DH, n_t, iblk).transpose(1, 0, 2)
    entries = width * 3 * DH * n_t
    dma = pltpu.SemaphoreType.DMA
    anywhere = pl.BlockSpec(memory_space=pl.ANY)
    vmem = pl.BlockSpec(memory_space=pltpu.VMEM)
    smem = pl.BlockSpec(memory_space=pltpu.SMEM)
    z = n_seq - 1
    input_t, weight_t = pl.pallas_call(
        functools.partial(kernel, n_seq, n_t, entries, aligned),
        out_shape=(
            jax.ShapeDtypeStruct((rows, iblk), BF16),
            jax.ShapeDtypeStruct((3 * DH, blk), BF16),
        ),
        in_specs=[anywhere, anywhere, anywhere, vmem, smem, smem],
        out_specs=(vmem, vmem),
        scratch_shapes=[
            pltpu.VMEM((rows, width), BF16),
            pltpu.VMEM((3 * DH, width), BF16),
            pltpu.VMEM(w_b.shape, BF16),
            pltpu.VMEM((z, rows, blk), BF16),
            pltpu.VMEM((rows, 3 * DH), BF16),
            pltpu.VMEM((n_seq, 3 * DH, rows), BF16),
            pltpu.VMEM((2, n_seq, DH, DH), BF16),
            pltpu.VMEM((nc, rows, iblk), BF16),
            pltpu.VMEM((nc, rows, iblk), BF16),
            pltpu.VMEM((nc - 1, rows, iblk), BF16),
            pltpu.VMEM((nc - 1, rows, iblk), BF16),
            pltpu.VMEM((3 * DH, blk), F32),
            pltpu.VMEM((n_seq, 8, 128), F32),
            pltpu.VMEM((n_t, 8, 128), F32),
            dma((2 * LOAD_CHUNKS + 1,)),
            dma((z,)), dma((z,)),
            dma((z, 3)), dma((z, 3)),
            dma((z,)), dma((z,)),
            dma((z,)), dma((z,)),
            dma((z,)), dma((z,)),
            dma((nc,)), dma((nc,)),
            dma((nc - 1,)), dma((nc - 1,)),
            dma((z,)), dma((z,)),
            dma((n_t - 1,)), dma((n_t - 1,)),
        ],
        compiler_params=pltpu.CompilerParams(
            collective_id=0, has_side_effects=True, vmem_limit_bytes=48 * 1024 * 1024
        ),
    )(layer_inputs, w_t, w_b, result_sensitivity, rate, events)
    weight_grad = weight_t.reshape(3, DH, blk).transpose(2, 0, 1)
    return input_t.T, weight_grad


def solution(mesh):
    return jax.shard_map(
        functools.partial(body, mesh.shape["seq"], mesh.shape["tensor"]),
        mesh=mesh,
        in_specs=(P("seq", None), P(None, None, "tensor"), P("seq", "tensor"), P("tensor"), P()),
        out_specs=(P("tensor", "seq"), P("seq", None, "tensor")),
        check_vma=False,
    )
```

```python
import functools
import math

import jax
import jax.numpy as jnp
from jax import lax
from jax.experimental import pallas as pl
from jax.experimental.pallas import tpu as pltpu
from jax.sharding import PartitionSpec as P

DH = 96
DROP_LOGARITHM = 0.3
CLIP_RMS = 0.5
MESH = pl.DeviceIdType.MESH
F32 = jnp.float32
BF16 = jnp.bfloat16
LOAD_CHUNKS = 4


def mm(a, b):
    return jnp.dot(a, b, preferred_element_type=F32)


def mm_nt(a, b):
    return lax.dot_general(a, b, (((1,), (1,)), ((), ())), preferred_element_type=F32)


def kernel(
    n_seq, n_t, entries, aligned, flat,
    x_hbm, w_hbm, wb_hbm, o_hbm, rate_hbm, events_hbm,
    ig_ref, wg_ref,
    x, w, wb, o_ref, rate_ref, events_ref,
    xg, g, gx, gt, st, ps, rc, sd, rd, acc, sqz, sqt,
    load_sem, small_sem, bx1s, bx1r, bx2s, bx2r, bx3s, bx3r, sts, str_, gs, gr,
    pss, psr, rds, rdr, zs, zr, ts, tr,
):
    rows, width = x_hbm.shape
    blk = width // n_seq
    iblk = width // n_t
    scale = DH ** (-0.5)
    s = lax.axis_index("seq")
    j = lax.axis_index("tensor")
    nc = n_t // 2
    k = lax.rem(j, 2)
    chip = j // 2
    sibling = j + 1 - 2 * k
    group = (j // 8) * 8
    c = lax.rem(j, 8) // 2
    q = blk // 4
    half = rows // 2

    wide = width // LOAD_CHUNKS
    loads = []
    for i in range(LOAD_CHUNKS):
        cols = pl.ds(i * wide, wide)
        for n, (src, dst) in enumerate(((x_hbm, x), (w_hbm, w))):
            copy = pltpu.make_async_copy(src.at[:, cols], dst.at[:, cols], load_sem.at[2 * i + n])
            copy.start()
            loads.append(copy)
    smalls = []
    for n, (src, dst) in enumerate(((o_hbm, o_ref), (rate_hbm, rate_ref), (events_hbm, events_ref))):
        copy = pltpu.make_async_copy(src, dst, small_sem.at[n])
        copy.start()
        smalls.append(copy)
    if not aligned:
        wb_copy = pltpu.make_async_copy(wb_hbm, wb, load_sem.at[2 * LOAD_CHUNKS])
        wb_copy.start()

    def seq_peer(d):
        return lax.rem(s + d, n_seq)

    def t_peer(d):
        return lax.rem(j + d, n_t)

    offsets = [(a, b) for a in range(n_seq) for b in range(n_t) if (flat or a * b == 0) and a + b]
    barrier = pltpu.get_barrier_semaphore()
    for a, b in offsets:
        pl.semaphore_signal(barrier, inc=1, device_id=(seq_peer(a), t_peer(b)), device_id_type=MESH)
    pl.semaphore_wait(barrier, len(offsets))

    sends = []

    def send(src, dst, ssem, rsem, device):
        copy = pltpu.make_async_remote_copy(
            src_ref=src, dst_ref=dst, send_sem=ssem, recv_sem=rsem,
            device_id=device, device_id_type=MESH,
        )
        copy.start()
        sends.append(copy)

    def wait_recv(ref, ssem, rsem, device):
        pltpu.make_async_remote_copy(
            src_ref=ref, dst_ref=ref, send_sem=ssem, recv_sem=rsem,
            device_id=device, device_id_type=MESH,
        ).wait_recv()

    def piece(d, core, chip_col):
        return xg.at[
            d - 1,
            pl.ds(pl.multiple_of(core * half, 32), half),
            pl.ds(pl.multiple_of(chip_col * q, 128), q),
        ]

    def token_half(d, core):
        return xg.at[d - 1, pl.ds(pl.multiple_of(core * half, 32), half), :]

    for d in range(1, n_seq):
        src = x_hbm.at[
            pl.ds(pl.multiple_of(k * half, 32), half),
            pl.ds(pl.multiple_of(seq_peer(d) * blk + c * q, 128), q),
        ]
        send(src, piece(d, k, c), bx1s.at[d - 1], bx1r.at[d - 1], (seq_peer(d), j))

    proj = jnp.zeros((3 * DH, rows), F32)
    for i in range(LOAD_CHUNKS):
        cols = pl.ds(i * wide, wide)
        loads[2 * i].wait()
        loads[2 * i + 1].wait()
        proj = proj + mm_nt(w[:, cols], x[:, cols])
    q_t = (proj[:DH] * scale).astype(BF16)
    k_t = proj[DH : 2 * DH].astype(BF16)
    v_t = proj[2 * DH :].astype(BF16)
    for copy in smalls:
        copy.wait()
    o = o_ref[...]
    o_t = o.astype(F32).T.astype(BF16)
    q_r = q_t.astype(F32).T.astype(BF16)
    v_r = v_t.astype(F32).T.astype(BF16)

    rate = rate_ref[0]
    n_events = events_ref.shape[0]
    base = s * rows
    lane = lax.broadcasted_iota(jnp.int32, (1, rows), 1)

    def events_in(low, high):
        total = jnp.zeros(jnp.broadcast_shapes(jnp.shape(low), jnp.shape(high)), F32)
        for n in range(n_events):
            e = events_ref[n]
            total = total + jnp.where((e > low) & (e <= high), 1.0, 0.0)
        return total

    last = jnp.full((1, rows), rows - 1, jnp.int32) + base
    before = jnp.full((1, rows), -1, jnp.int32) + base
    here = lane + base
    head_w = jnp.exp(-(rate * (lane + 1).astype(F32) + DROP_LOGARITHM * events_in(before, here)))
    tail_w = jnp.exp(
        -(rate * (rows - 1 - lane).astype(F32) + DROP_LOGARITHM * events_in(here, last))
    )

    st[0, 0] = mm((k_t.astype(F32) * tail_w).astype(BF16), v_r).astype(BF16)
    st[1, 0] = mm((q_t.astype(F32) * head_w).astype(BF16), o).astype(BF16)
    for d in range(1, n_seq):
        earlier = jnp.where(seq_peer(d) < s, 1, 0)
        send(st.at[earlier, 0], st.at[0, d], sts.at[d - 1], str_.at[d - 1], (seq_peer(d), j))

    for d in range(1, n_seq):
        wait_recv(piece(d, k, c), bx1s.at[d - 1], bx1r.at[d - 1], (s, j))
        for m in range(1, 4):
            to = group + 2 * lax.rem(c + m, 4) + k
            mine = piece(d, k, c)
            send(mine, mine, bx2s.at[d - 1, m - 1], bx2r.at[d - 1, m - 1], (s, to))

    t_idx = lax.broadcasted_iota(jnp.int32, (rows, rows), 0)
    s_idx = lax.broadcasted_iota(jnp.int32, (rows, rows), 1)
    decay = rate * (t_idx - s_idx).astype(F32) + DROP_LOGARITHM * events_in(
        s_idx + base, t_idx + base
    )
    weight = jnp.where(t_idx >= s_idx, jnp.exp(-jnp.maximum(decay, 0.0)), 0.0)
    scores = (mm(q_r, k_t) * weight).astype(BF16)
    dscores = (mm(o, v_t) * weight).astype(BF16)
    dq_t = mm_nt(k_t, dscores)
    dk_t = mm(q_t, dscores)
    dv_t = mm(o_t, scores)

    prefix = jnp.zeros((DH, DH), F32)
    suffix = jnp.zeros((DH, DH), F32)
    zero = jnp.zeros((1, DH), jnp.int32)
    for d in range(1, n_seq):
        wait_recv(st.at[0, d], sts.at[d - 1], str_.at[d - 1], (s, j))
        src = lax.rem(s + n_seq - d, n_seq)
        state = st[0, d].astype(F32)
        low = jnp.minimum(src, s)
        high = jnp.maximum(src, s)
        gap = rate * ((high - low - 1) * rows).astype(F32) + DROP_LOGARITHM * events_in(
            zero + ((low + 1) * rows - 1), zero + (high * rows - 1)
        )
        state = state * jnp.exp(-gap)
        is_fwd = (zero + src) < (zero + s)
        prefix = prefix + jnp.where(is_fwd, state, 0.0)
        suffix = suffix + jnp.where(is_fwd, 0.0, state)
    dq_t = dq_t + mm(prefix.astype(BF16), o_t) * head_w
    dk_t = dk_t + mm(suffix.astype(BF16), v_t) * tail_w
    dv_t = dv_t + mm(suffix.T.astype(BF16), k_t) * tail_w
    grads_t = jnp.concatenate([dq_t * scale, dk_t, dv_t], axis=0)
    gt[0] = grads_t.astype(BF16)
    g[...] = grads_t.T.astype(BF16)
    head, tail = 128, rows - 128
    low, high = grads_t[: 3 * DH // 2, head:], grads_t[3 * DH // 2 :, head:]
    gx[0, : 3 * DH] = grads_t[:, :head].astype(BF16)
    gx[0, 3 * DH :] = jnp.concatenate([low, high], axis=1).astype(BF16)
    for d in range(1, n_seq):
        send(gx.at[0], gx.at[d], gs.at[d - 1], gr.at[d - 1], (seq_peer(d), j))

    step = 256 if iblk % 256 == 0 else iblk
    if not aligned:
        wb_copy.wait()

    def block_term(owner, put):
        if aligned:
            def one(i, carry):
                cols = pl.ds(pl.multiple_of(owner * iblk + i * step, 128), step)
                put(pl.ds(pl.multiple_of(i * step, 128), step), mm(g[...], w[:, cols]))
                return carry
            lax.fori_loop(0, iblk // step, one, 0)
        else:
            put(pl.ds(0, iblk), mm(g[...], wb[owner]))

    for m in range(1, nc + 1):
        to_chip = lax.rem(chip + m, nc)
        def put(cols, value, m=m):
            ps[m - 1, :, cols] = value.astype(BF16)
        block_term(2 * to_chip + 1 - k, put)
        send(ps.at[m - 1], rc.at[m - 1], pss.at[m - 1], psr.at[m - 1], (s, sibling))

    for m in range(1, nc):
        wait_recv(rc.at[m - 1], pss.at[m - 1], psr.at[m - 1], (s, sibling))
        to_chip = lax.rem(chip + m, nc)
        def put(cols, value, m=m):
            sd[m - 1, :, cols] = (value + rc[m - 1, :, cols].astype(F32)).astype(BF16)
        block_term(2 * to_chip + k, put)
        send(sd.at[m - 1], rd.at[m - 1], rds.at[m - 1], rdr.at[m - 1], (s, 2 * to_chip + k))

    for d in range(1, n_seq):
        for m in range(1, 4):
            wait_recv(
                piece(d, k, lax.rem(c + 4 - m, 4)),
                bx2s.at[d - 1, m - 1], bx2r.at[d - 1, m - 1], (s, j),
            )
        send(token_half(d, k), token_half(d, k), bx3s.at[d - 1], bx3r.at[d - 1], (s, sibling))

    wstep = 256
    for d in range(1, n_seq):
        wait_recv(token_half(d, 1 - k), bx3s.at[d - 1], bx3r.at[d - 1], (s, sibling))
        wait_recv(gx.at[d], gs.at[d - 1], gr.at[d - 1], (s, j))
        gt[d, :, :head] = gx[d, : 3 * DH]
        packed = gx[d, 3 * DH :].astype(F32)
        gt[d, : 3 * DH // 2, head:] = packed[:, :tail].astype(BF16)
        gt[d, 3 * DH // 2 :, head:] = packed[:, tail:].astype(BF16)

    def grad_cols(i, square):
        cols = pl.ds(pl.multiple_of(i * wstep, 128), wstep)
        total = mm(gt[0], x[:, pl.ds(pl.multiple_of(s * blk + i * wstep, 128), wstep)])
        for d in range(1, n_seq):
            total = total + mm(gt[d], xg[d - 1, :, cols])
        acc[:, cols] = total
        return square + jnp.sum((total * total).reshape(3 * DH // 8, 8, wstep), axis=0)

    square = lax.fori_loop(0, blk // wstep, grad_cols, jnp.zeros((8, wstep), F32))
    sqt[0] = square[:, :128] + square[:, 128:]
    if flat:
        for i, (a, b) in enumerate(offsets):
            to = (seq_peer(a), t_peer(b))
            send(sqt.at[0], sqt.at[i + 1], ts.at[i], tr.at[i], to)
    else:
        sqz[0] = sqt[0]
        for d in range(1, n_seq):
            send(sqz.at[0], sqz.at[d], zs.at[d - 1], zr.at[d - 1], (seq_peer(d), j))

    wait_recv(rc.at[nc - 1], pss.at[nc - 1], psr.at[nc - 1], (s, sibling))
    for m in range(1, nc):
        wait_recv(rd.at[m - 1], rds.at[m - 1], rdr.at[m - 1], (s, j))

    def put(cols, value):
        total = value + rc[nc - 1, :, cols].astype(F32)
        for m in range(1, nc):
            total = total + rd[m - 1, :, cols].astype(F32)
        ig_ref[:, cols] = total.astype(BF16)

    if flat:
        block_term(j, put)
        peers = len(offsets)
    else:
        for d in range(1, n_seq):
            wait_recv(sqz.at[d], zs.at[d - 1], zr.at[d - 1], (s, j))
        total = sqz[0]
        for d in range(1, n_seq):
            total = total + sqz[d]
        sqt[0] = total
        for d in range(1, n_t):
            send(sqt.at[0], sqt.at[d], ts.at[d - 1], tr.at[d - 1], (s, t_peer(d)))
        block_term(j, put)
        peers = n_t - 1
    for i in range(peers):
        wait_recv(sqt.at[i + 1], ts.at[i], tr.at[i], (s, j))
    total = sqt[0]
    for i in range(peers):
        total = total + sqt[i + 1]
    total = jnp.sum(jnp.sum(total, axis=1, keepdims=True), axis=0, keepdims=True)
    factor = jnp.minimum(1.0, CLIP_RMS * math.sqrt(entries) / jnp.sqrt(total + 1e-06))

    def scaled(i, carry):
        cols = pl.ds(pl.multiple_of(i * wstep, 128), wstep)
        wg_ref[:, cols] = (acc[:, cols] * factor).astype(BF16)
        return carry

    lax.fori_loop(0, blk // wstep, scaled, 0)
    for copy in sends:
        copy.wait_send()


def body(n_seq, n_t, layer_inputs, projection_matrices, result_sensitivity, rate, events):
    rows, width = layer_inputs.shape
    blk, iblk, nc = width // n_seq, width // n_t, n_t // 2
    aligned = iblk % 128 == 0
    w_t = projection_matrices.transpose(1, 2, 0).reshape(3 * DH, width)
    if aligned:
        w_b = jnp.zeros((1, 8, 128), BF16)
    else:
        w_b = w_t.reshape(3 * DH, n_t, iblk).transpose(1, 0, 2)
    entries = width * 3 * DH * n_t
    flat = n_seq * n_t <= 64
    peers = n_seq * n_t - 1 if flat else n_t - 1
    dma = pltpu.SemaphoreType.DMA
    anywhere = pl.BlockSpec(memory_space=pl.ANY)
    vmem = pl.BlockSpec(memory_space=pltpu.VMEM)
    z = n_seq - 1
    input_t, weight_t = pl.pallas_call(
        functools.partial(kernel, n_seq, n_t, entries, aligned, flat),
        out_shape=(
            jax.ShapeDtypeStruct((rows, iblk), BF16),
            jax.ShapeDtypeStruct((3 * DH, blk), BF16),
        ),
        in_specs=[anywhere] * 6,
        out_specs=(vmem, vmem),
        scratch_shapes=[
            pltpu.VMEM((rows, width), BF16),
            pltpu.VMEM((3 * DH, width), BF16),
            pltpu.VMEM(w_b.shape, BF16),
            pltpu.VMEM(result_sensitivity.shape, BF16),
            pltpu.SMEM(rate.shape, F32),
            pltpu.SMEM(events.shape, jnp.int32),
            pltpu.VMEM((z, rows, blk), BF16),
            pltpu.VMEM((rows, 3 * DH), BF16),
            pltpu.VMEM((n_seq, 9 * DH // 2, 128), BF16),
            pltpu.VMEM((n_seq, 3 * DH, rows), BF16),
            pltpu.VMEM((2, n_seq, DH, DH), BF16),
            pltpu.VMEM((nc, rows, iblk), BF16),
            pltpu.VMEM((nc, rows, iblk), BF16),
            pltpu.VMEM((nc - 1, rows, iblk), BF16),
            pltpu.VMEM((nc - 1, rows, iblk), BF16),
            pltpu.VMEM((3 * DH, blk), F32),
            pltpu.VMEM((n_seq, 8, 128), F32),
            pltpu.VMEM((peers + 1, 8, 128), F32),
            dma((2 * LOAD_CHUNKS + 1,)), dma((3,)),
            dma((z,)), dma((z,)),
            dma((z, 3)), dma((z, 3)),
            dma((z,)), dma((z,)),
            dma((z,)), dma((z,)),
            dma((z,)), dma((z,)),
            dma((nc,)), dma((nc,)),
            dma((nc - 1,)), dma((nc - 1,)),
            dma((z,)), dma((z,)),
            dma((peers,)), dma((peers,)),
        ],
        compiler_params=pltpu.CompilerParams(
            collective_id=0, has_side_effects=True, vmem_limit_bytes=60 * 1024 * 1024
        ),
    )(layer_inputs, w_t, w_b, result_sensitivity, rate, events)
    weight_grad = weight_t.reshape(3, DH, blk).transpose(2, 0, 1)
    return input_t.T, weight_grad


def solution(mesh):
    return jax.shard_map(
        functools.partial(body, mesh.shape["seq"], mesh.shape["tensor"]),
        mesh=mesh,
        in_specs=(P("seq", None), P(None, None, "tensor"), P("seq", "tensor"), P("tensor"), P()),
        out_specs=(P("tensor", "seq"), P("seq", None, "tensor")),
        check_vma=False,
    )
```

```python
import functools
import math

import jax
import jax.numpy as jnp
from jax import lax
from jax.experimental import pallas as pl
from jax.experimental.pallas import tpu as pltpu
from jax.sharding import PartitionSpec as P

DH = 96
DROP_LOGARITHM = 0.3
CLIP_RMS = 0.5
MESH = pl.DeviceIdType.MESH
F32 = jnp.float32
BF16 = jnp.bfloat16
LOAD_CHUNKS = 4


def mm(a, b):
    return jnp.dot(a, b, preferred_element_type=F32)


def mm_nt(a, b):
    return lax.dot_general(a, b, (((1,), (1,)), ((), ())), preferred_element_type=F32)


def kernel(
    n_seq, n_t, entries, aligned, flat,
    x_hbm, w_hbm, wb_hbm, o_hbm, rate_hbm, events_hbm,
    ig_ref, wg_ref,
    x, w, wb, o_ref, rate_ref, events_ref,
    xg, g, gx, gt, st, ps, rc, sd, rt, rd, own, acc, sqz, sqt,
    load_sem, small_sem, bx1s, bx1r, bx2s, bx2r, bx3s, bx3r, bx4s, bx4r, sts, str_, gs, gr,
    pss, psr, rds, rdr, zs, zr, ts, tr,
):
    rows, width = x_hbm.shape
    blk = width // n_seq
    iblk = width // n_t
    scale = DH ** (-0.5)
    s = lax.axis_index("seq")
    j = lax.axis_index("tensor")
    nc = n_t // 2
    k = lax.rem(j, 2)
    chip = j // 2
    sibling = j + 1 - 2 * k
    group = (j // 8) * 8
    c = lax.rem(j, 8) // 2
    q = blk // 4
    half = rows // 2
    order = sorted(range(1, n_seq), key=lambda d: min(d, n_seq - d))
    first, rest = order[: max(1, n_seq // 2)], order[max(1, n_seq // 2) :]

    def across(n):
        a, b = lax.rem(n, 2), lax.rem(n // 2, 2)
        return n + 1 - 2 * a, n + 2 - 4 * b, n + 3 - 2 * a - 4 * b

    c_x, c_y, c_d = across(c)
    dev_x, dev_y = group + 2 * c_x + k, group + 2 * c_y + k

    wide = width // LOAD_CHUNKS
    loads = []
    for i in range(LOAD_CHUNKS):
        cols = pl.ds(i * wide, wide)
        for n, (src, dst) in enumerate(((x_hbm, x), (w_hbm, w))):
            copy = pltpu.make_async_copy(src.at[:, cols], dst.at[:, cols], load_sem.at[2 * i + n])
            copy.start()
            loads.append(copy)
    smalls = []
    for n, (src, dst) in enumerate(((o_hbm, o_ref), (rate_hbm, rate_ref), (events_hbm, events_ref))):
        copy = pltpu.make_async_copy(src, dst, small_sem.at[n])
        copy.start()
        smalls.append(copy)
    if not aligned:
        wb_copy = pltpu.make_async_copy(wb_hbm, wb, load_sem.at[2 * LOAD_CHUNKS])
        wb_copy.start()

    def seq_peer(d):
        return lax.rem(s + d, n_seq)

    def t_peer(d):
        return lax.rem(j + d, n_t)

    offsets = [(a, b) for a in range(n_seq) for b in range(n_t) if (flat or a * b == 0) and a + b]
    barrier = pltpu.get_barrier_semaphore()
    for a, b in offsets:
        pl.semaphore_signal(barrier, inc=1, device_id=(seq_peer(a), t_peer(b)), device_id_type=MESH)
    pl.semaphore_wait(barrier, len(offsets))

    sends = []

    def send(src, dst, ssem, rsem, device):
        copy = pltpu.make_async_remote_copy(
            src_ref=src, dst_ref=dst, send_sem=ssem, recv_sem=rsem,
            device_id=device, device_id_type=MESH,
        )
        copy.start()
        sends.append(copy)

    def wait_recv(ref, ssem, rsem, device):
        pltpu.make_async_remote_copy(
            src_ref=ref, dst_ref=ref, send_sem=ssem, recv_sem=rsem,
            device_id=device, device_id_type=MESH,
        ).wait_recv()

    def piece(d, core, chip_col):
        return xg.at[
            d - 1,
            pl.ds(pl.multiple_of(core * half, 32), half),
            pl.ds(pl.multiple_of(chip_col * q, 128), q),
        ]

    def quarter(d, chip_col, low):
        start = pl.multiple_of(k * half + low * (half // 2), 16)
        return xg.at[d - 1, pl.ds(start, half // 2), pl.ds(pl.multiple_of(chip_col * q, 128), q)]

    def share(d):
        wait_recv(piece(d, k, c), bx1s.at[d - 1], bx1r.at[d - 1], (s, j))
        mine = piece(d, k, c)
        send(mine, mine, bx2s.at[d - 1, 0], bx2r.at[d - 1, 0], (s, dev_x))
        send(mine, mine, bx2s.at[d - 1, 1], bx2r.at[d - 1, 1], (s, dev_y))

    def forward(d):
        wait_recv(piece(d, k, c_x), bx2s.at[d - 1, 0], bx2r.at[d - 1, 0], (s, dev_x))
        top = quarter(d, c_x, 0)
        send(top, top, bx4s.at[d - 1, 0], bx4r.at[d - 1, 0], (s, dev_y))
        wait_recv(piece(d, k, c_y), bx2s.at[d - 1, 1], bx2r.at[d - 1, 1], (s, dev_y))
        bottom = quarter(d, c_y, 1)
        send(bottom, bottom, bx4s.at[d - 1, 1], bx4r.at[d - 1, 1], (s, dev_x))

    def meet(d):
        wait_recv(quarter(d, c_d, 0), bx4s.at[d - 1, 0], bx4r.at[d - 1, 0], (s, dev_y))
        wait_recv(quarter(d, c_d, 1), bx4s.at[d - 1, 1], bx4r.at[d - 1, 1], (s, dev_x))
        send(token_half(d, k), token_half(d, k), bx3s.at[d - 1], bx3r.at[d - 1], (s, sibling))

    def token_half(d, core):
        return xg.at[d - 1, pl.ds(pl.multiple_of(core * half, 32), half), :]

    def exchange(d):
        src = x_hbm.at[
            pl.ds(pl.multiple_of(k * half, 32), half),
            pl.ds(pl.multiple_of(seq_peer(d) * blk + c * q, 128), q),
        ]
        send(src, piece(d, k, c), bx1s.at[d - 1], bx1r.at[d - 1], (seq_peer(d), j))

    for d in first:
        exchange(d)

    proj = jnp.zeros((3 * DH, rows), F32)
    for i in range(LOAD_CHUNKS):
        cols = pl.ds(i * wide, wide)
        loads[2 * i].wait()
        loads[2 * i + 1].wait()
        proj = proj + mm_nt(w[:, cols], x[:, cols])
    q_t = (proj[:DH] * scale).astype(BF16)
    k_t = proj[DH : 2 * DH].astype(BF16)
    v_t = proj[2 * DH :].astype(BF16)
    for copy in smalls:
        copy.wait()
    o = o_ref[...]
    o_t = o.astype(F32).T.astype(BF16)
    q_r = q_t.astype(F32).T.astype(BF16)
    v_r = v_t.astype(F32).T.astype(BF16)

    rate = rate_ref[0]
    n_events = events_ref.shape[0]
    base = s * rows
    lane = lax.broadcasted_iota(jnp.int32, (1, rows), 1)

    def events_in(low, high):
        total = jnp.zeros(jnp.broadcast_shapes(jnp.shape(low), jnp.shape(high)), F32)
        for n in range(n_events):
            e = events_ref[n]
            total = total + jnp.where((e > low) & (e <= high), 1.0, 0.0)
        return total

    last = jnp.full((1, rows), rows - 1, jnp.int32) + base
    before = jnp.full((1, rows), -1, jnp.int32) + base
    here = lane + base
    head_w = jnp.exp(-(rate * (lane + 1).astype(F32) + DROP_LOGARITHM * events_in(before, here)))
    tail_w = jnp.exp(
        -(rate * (rows - 1 - lane).astype(F32) + DROP_LOGARITHM * events_in(here, last))
    )

    st[0, 0] = mm((k_t.astype(F32) * tail_w).astype(BF16), v_r).astype(BF16)
    st[1, 0] = mm((q_t.astype(F32) * head_w).astype(BF16), o).astype(BF16)
    for d in range(1, n_seq):
        earlier = jnp.where(seq_peer(d) < s, 1, 0)
        send(st.at[earlier, 0], st.at[0, d], sts.at[d - 1], str_.at[d - 1], (seq_peer(d), j))

    for d in rest:
        exchange(d)

    t_idx = lax.broadcasted_iota(jnp.int32, (rows, rows), 0)
    s_idx = lax.broadcasted_iota(jnp.int32, (rows, rows), 1)
    decay = rate * (t_idx - s_idx).astype(F32) + DROP_LOGARITHM * events_in(
        s_idx + base, t_idx + base
    )
    weight = jnp.where(t_idx >= s_idx, jnp.exp(-jnp.maximum(decay, 0.0)), 0.0)
    scores = (mm(q_r, k_t) * weight).astype(BF16)
    dscores = (mm(o, v_t) * weight).astype(BF16)
    for d in first:
        share(d)
    dq_t = mm_nt(k_t, dscores)
    dk_t = mm(q_t, dscores)
    dv_t = mm(o_t, scores)

    prefix = jnp.zeros((DH, DH), F32)
    suffix = jnp.zeros((DH, DH), F32)
    zero = jnp.zeros((1, DH), jnp.int32)
    for d in range(1, n_seq):
        wait_recv(st.at[0, d], sts.at[d - 1], str_.at[d - 1], (s, j))
        src = lax.rem(s + n_seq - d, n_seq)
        state = st[0, d].astype(F32)
        low = jnp.minimum(src, s)
        high = jnp.maximum(src, s)
        gap = rate * ((high - low - 1) * rows).astype(F32) + DROP_LOGARITHM * events_in(
            zero + ((low + 1) * rows - 1), zero + (high * rows - 1)
        )
        state = state * jnp.exp(-gap)
        is_fwd = (zero + src) < (zero + s)
        prefix = prefix + jnp.where(is_fwd, state, 0.0)
        suffix = suffix + jnp.where(is_fwd, 0.0, state)
    dq_t = dq_t + mm(prefix.astype(BF16), o_t) * head_w
    dk_t = dk_t + mm(suffix.astype(BF16), v_t) * tail_w
    dv_t = dv_t + mm(suffix.T.astype(BF16), k_t) * tail_w
    grads_t = jnp.concatenate([dq_t * scale, dk_t, dv_t], axis=0)
    gt[0] = grads_t.astype(BF16)
    g[...] = grads_t.T.astype(BF16)
    head, tail = 128, rows - 128
    low, high = grads_t[: 3 * DH // 2, head:], grads_t[3 * DH // 2 :, head:]
    gx[0, : 3 * DH] = grads_t[:, :head].astype(BF16)
    gx[0, 3 * DH :] = jnp.concatenate([low, high], axis=1).astype(BF16)
    for d in range(1, n_seq):
        send(gx.at[0], gx.at[d], gs.at[d - 1], gr.at[d - 1], (seq_peer(d), j))

    step = 256 if iblk % 256 == 0 else iblk
    if not aligned:
        wb_copy.wait()

    def block_term(owner, put):
        if aligned:
            def one(i, carry):
                cols = pl.ds(pl.multiple_of(owner * iblk + i * step, 128), step)
                put(pl.ds(pl.multiple_of(i * step, 128), step), mm(g[...], w[:, cols]))
                return carry
            lax.fori_loop(0, iblk // step, one, 0)
        else:
            put(pl.ds(0, iblk), mm(g[...], wb[owner]))

    if nc == 4:
        chip_x, chip_y, chip_d = across(chip)
        chips = [chip_d, chip_x, chip_y, chip]
    else:
        chips = [lax.rem(chip + m, nc) for m in range(1, nc + 1)]
    for m in range(nc):
        def put(cols, value, m=m):
            ps[m, :, cols] = value.astype(BF16)
        block_term(2 * chips[m] + 1 - k, put)
        send(ps.at[m], rc.at[m], pss.at[m], psr.at[m], (s, sibling))
    for d in rest:
        share(d)

    def pair_sum(m, put):
        wait_recv(rc.at[m], pss.at[m], psr.at[m], (s, sibling))
        def put_sum(cols, value):
            put(cols, value + rc[m, :, cols].astype(F32))
        block_term(2 * chips[m] + k, put_sum)

    if nc == 4:
        to_x, to_y = (s, 2 * chip_x + k), (s, 2 * chip_y + k)
        top, bottom = pl.ds(0, half), pl.ds(half, half)
        targets = [
            (rt.at[0], to_x), (rt.at[1], to_y),
            (rd.at[0, top], to_x), (rd.at[1, bottom], to_y),
            (rd.at[0, bottom], to_x), (rd.at[1, top], to_y),
        ]

        def send_part(n):
            send(sd.at[n], targets[n][0], rds.at[n], rdr.at[n], targets[n][1])

        def wait_part(n):
            wait_recv(targets[n][0], rds.at[n], rdr.at[n], targets[n][1])

        for m, (a, b) in enumerate(((0, 1), (2, 4), (5, 3))):
            def put(cols, value, a=a, b=b):
                sd[a, :, cols] = value[:half].astype(BF16)
                sd[b, :, cols] = value[half:].astype(BF16)
            pair_sum(m, put)
            for n in (a, b):
                if n < 4:
                    send_part(n)
        for d in first:
            forward(d)
        for n, got in ((4, 1), (5, 0)):
            wait_part(got)
            sd[n] = (sd[n].astype(F32) + rt[got].astype(F32)).astype(BF16)
            send_part(n)
        arrivals = 2
    else:
        for m in range(nc - 1):
            def put(cols, value, m=m):
                sd[m, :, cols] = value.astype(BF16)
            pair_sum(m, put)
            send(sd.at[m], rd.at[m], rds.at[m], rdr.at[m], (s, 2 * chips[m] + k))
        for d in first:
            forward(d)
        arrivals = nc - 1
    for d in rest:
        forward(d)
    for d in order:
        meet(d)

    def put(cols, value):
        own[:, cols] = value
    pair_sum(nc - 1, put)

    wstep = 256

    def grad_cols(slot, is_last, i, square):
        cols = pl.ds(pl.multiple_of(i * wstep, 128), wstep)
        if slot == 0:
            acc[:, cols] = mm(gt[0], x[:, pl.ds(pl.multiple_of(s * blk + i * wstep, 128), wstep)])
            return square
        total = acc[:, cols] + mm(gt[slot], xg[slot - 1, :, cols])
        acc[:, cols] = total
        if is_last:
            square = square + jnp.sum((total * total).reshape(3 * DH // 8, 8, wstep), axis=0)
        return square

    square = jnp.zeros((8, wstep), F32)
    for d in [0] + order:
        if d:
            wait_recv(gx.at[d], gs.at[d - 1], gr.at[d - 1], (s, j))
            gt[d, :, :head] = gx[d, : 3 * DH]
            packed = gx[d, 3 * DH :].astype(F32)
            gt[d, : 3 * DH // 2, head:] = packed[:, :tail].astype(BF16)
            gt[d, 3 * DH // 2 :, head:] = packed[:, tail:].astype(BF16)
            wait_recv(token_half(d, 1 - k), bx3s.at[d - 1], bx3r.at[d - 1], (s, sibling))
        square = lax.fori_loop(
            0, blk // wstep, functools.partial(grad_cols, d, d == order[-1]), square
        )
    sqt[0] = square[:, :128] + square[:, 128:]
    if flat:
        for i, (a, b) in enumerate(offsets):
            to = (seq_peer(a), t_peer(b))
            send(sqt.at[0], sqt.at[i + 1], ts.at[i], tr.at[i], to)
    else:
        sqz[0] = sqt[0]
        for d in range(1, n_seq):
            send(sqz.at[0], sqz.at[d], zs.at[d - 1], zr.at[d - 1], (seq_peer(d), j))

    def finish():
        if nc == 4:
            for n in range(2, 6):
                wait_part(n)
        else:
            for m in range(arrivals):
                wait_recv(rd.at[m], rds.at[m], rdr.at[m], (s, j))
        total = own[...]
        for m in range(arrivals):
            total = total + rd[m].astype(F32)
        ig_ref[...] = total.astype(BF16)

    if flat:
        finish()
        peers = len(offsets)
    else:
        for d in range(1, n_seq):
            wait_recv(sqz.at[d], zs.at[d - 1], zr.at[d - 1], (s, j))
        total = sqz[0]
        for d in range(1, n_seq):
            total = total + sqz[d]
        sqt[0] = total
        for d in range(1, n_t):
            send(sqt.at[0], sqt.at[d], ts.at[d - 1], tr.at[d - 1], (s, t_peer(d)))
        finish()
        peers = n_t - 1
    for i in range(peers):
        wait_recv(sqt.at[i + 1], ts.at[i], tr.at[i], (s, j))
    total = sqt[0]
    for i in range(peers):
        total = total + sqt[i + 1]
    total = jnp.sum(jnp.sum(total, axis=1, keepdims=True), axis=0, keepdims=True)
    factor = jnp.minimum(1.0, CLIP_RMS * math.sqrt(entries) / jnp.sqrt(total + 1e-06))

    def scaled(i, carry):
        cols = pl.ds(pl.multiple_of(i * wstep, 128), wstep)
        wg_ref[:, cols] = (acc[:, cols] * factor).astype(BF16)
        return carry

    lax.fori_loop(0, blk // wstep, scaled, 0)
    for copy in sends:
        copy.wait_send()


def body(n_seq, n_t, layer_inputs, projection_matrices, result_sensitivity, rate, events):
    rows, width = layer_inputs.shape
    blk, iblk, nc = width // n_seq, width // n_t, n_t // 2
    aligned = iblk % 128 == 0
    w_t = projection_matrices.transpose(1, 2, 0).reshape(3 * DH, width)
    if aligned:
        w_b = result_sensitivity
    else:
        w_b = w_t.reshape(3 * DH, n_t, iblk).transpose(1, 0, 2)
    entries = width * 3 * DH * n_t
    flat = n_seq * n_t <= 64
    peers = n_seq * n_t - 1 if flat else n_t - 1
    dma = pltpu.SemaphoreType.DMA
    vmem = pl.BlockSpec(memory_space=pltpu.VMEM)
    z = n_seq - 1
    input_t, weight_t = pl.pallas_call(
        functools.partial(kernel, n_seq, n_t, entries, aligned, flat),
        out_shape=(
            pltpu.VMEM((rows, iblk), BF16),
            pltpu.VMEM((3 * DH, blk), BF16),
        ),
        in_specs=[pl.BlockSpec(memory_space=pltpu.HBM)] * 6,
        out_specs=(vmem, vmem),
        scratch_shapes=[
            pltpu.VMEM((rows, width), BF16),
            pltpu.VMEM((3 * DH, width), BF16),
            pltpu.VMEM((8, 128) if aligned else w_b.shape, BF16),
            pltpu.VMEM(result_sensitivity.shape, BF16),
            pltpu.SMEM(rate.shape, F32),
            pltpu.SMEM(events.shape, jnp.int32),
            pltpu.VMEM((z, rows, blk), BF16),
            pltpu.VMEM((rows, 3 * DH), BF16),
            pltpu.VMEM((n_seq, 9 * DH // 2, 128), BF16),
            pltpu.VMEM((n_seq, 3 * DH, rows), BF16),
            pltpu.VMEM((2, n_seq, DH, DH), BF16),
            pltpu.VMEM((nc, rows, iblk), BF16),
            pltpu.VMEM((nc, rows, iblk), BF16),
            pltpu.VMEM((6, rows // 2, iblk) if nc == 4 else (nc - 1, rows, iblk), BF16),
            pltpu.VMEM((2, rows // 2, iblk), BF16),
            pltpu.VMEM((2 if nc == 4 else nc - 1, rows, iblk), BF16),
            pltpu.VMEM((rows, iblk), F32),
            pltpu.VMEM((3 * DH, blk), F32),
            pltpu.VMEM((n_seq, 8, 128), F32),
            pltpu.VMEM((peers + 1, 8, 128), F32),
            dma((2 * LOAD_CHUNKS + 1,)), dma((3,)),
            dma((z,)), dma((z,)),
            dma((z, 2)), dma((z, 2)),
            dma((z,)), dma((z,)),
            dma((z, 2)), dma((z, 2)),
            dma((z,)), dma((z,)),
            dma((z,)), dma((z,)),
            dma((nc,)), dma((nc,)),
            dma((6 if nc == 4 else nc - 1,)), dma((6 if nc == 4 else nc - 1,)),
            dma((z,)), dma((z,)),
            dma((peers,)), dma((peers,)),
        ],
        compiler_params=pltpu.CompilerParams(
            collective_id=0, has_side_effects=True, vmem_limit_bytes=60 * 1024 * 1024
        ),
    )(layer_inputs, w_t, w_b, result_sensitivity, rate, events)
    weight_grad = weight_t.reshape(3, DH, blk).transpose(2, 0, 1)
    return input_t.T, weight_grad


def solution(mesh):
    return jax.shard_map(
        functools.partial(body, mesh.shape["seq"], mesh.shape["tensor"]),
        mesh=mesh,
        in_specs=(P("seq", None), P(None, None, "tensor"), P("seq", "tensor"), P("tensor"), P()),
        out_specs=(P("tensor", "seq"), P("seq", None, "tensor")),
        check_vma=False,
    )
```

```python
import functools
import math

import jax
import jax.numpy as jnp
from jax import lax
from jax.experimental import pallas as pl
from jax.experimental.pallas import tpu as pltpu
from jax.sharding import PartitionSpec as P

DH = 96
DROP_LOGARITHM = 0.3
CLIP_RMS = 0.5
MESH = pl.DeviceIdType.MESH
F32 = jnp.float32
BF16 = jnp.bfloat16
LOAD_CHUNKS = 4


def mm(a, b):
    return jnp.dot(a, b, preferred_element_type=F32)


def mm_nt(a, b):
    return lax.dot_general(a, b, (((1,), (1,)), ((), ())), preferred_element_type=F32)


def kernel(
    n_seq, n_t, entries, aligned, flat,
    x_hbm, w_hbm, wb_hbm, o_hbm, rate_hbm, events_hbm,
    ig_ref, wg_ref,
    x, w, wb, o_ref, rate_ref, events_ref,
    xg, g, gx, gt, st, ps, rc, sd, rt, rd, own, acc, sqz, sqt,
    load_sem, small_sem, bx1s, bx1r, bx2s, bx2r, bx3s, bx3r, sts, str_, gs, gr,
    pss, psr, rds, rdr, zs, zr, ts, tr,
):
    rows, width = x_hbm.shape
    blk = width // n_seq
    iblk = width // n_t
    scale = DH ** (-0.5)
    s = lax.axis_index("seq")
    j = lax.axis_index("tensor")
    nc = n_t // 2
    k = lax.rem(j, 2)
    chip = j // 2
    sibling = j + 1 - 2 * k
    group = (j // 8) * 8
    c = lax.rem(j, 8) // 2
    q = blk // 4
    half = rows // 2
    order = sorted(range(1, n_seq), key=lambda d: min(d, n_seq - d))
    first, rest = order[: max(1, n_seq // 2)], order[max(1, n_seq // 2) :]

    def across(n):
        a, b = lax.rem(n, 2), lax.rem(n // 2, 2)
        return n + 1 - 2 * a, n + 2 - 4 * b, n + 3 - 2 * a - 4 * b

    c_x, c_y, c_d = across(c)
    dev_x, dev_y, dev_d = group + 2 * c_x + k, group + 2 * c_y + k, group + 2 * c_d + k

    wide = width // LOAD_CHUNKS
    loads = []
    for i in range(LOAD_CHUNKS):
        cols = pl.ds(i * wide, wide)
        for n, (src, dst) in enumerate(((x_hbm, x), (w_hbm, w))):
            copy = pltpu.make_async_copy(src.at[:, cols], dst.at[:, cols], load_sem.at[2 * i + n])
            copy.start()
            loads.append(copy)
    smalls = []
    for n, (src, dst) in enumerate(((o_hbm, o_ref), (rate_hbm, rate_ref), (events_hbm, events_ref))):
        copy = pltpu.make_async_copy(src, dst, small_sem.at[n])
        copy.start()
        smalls.append(copy)
    if not aligned:
        wb_copy = pltpu.make_async_copy(wb_hbm, wb, load_sem.at[2 * LOAD_CHUNKS])
        wb_copy.start()

    def seq_peer(d):
        return lax.rem(s + d, n_seq)

    def t_peer(d):
        return lax.rem(j + d, n_t)

    offsets = [(a, b) for a in range(n_seq) for b in range(n_t) if (flat or a * b == 0) and a + b]
    barrier = pltpu.get_barrier_semaphore()
    for a, b in offsets:
        pl.semaphore_signal(barrier, inc=1, device_id=(seq_peer(a), t_peer(b)), device_id_type=MESH)
    pl.semaphore_wait(barrier, len(offsets))

    sends = []

    def send(src, dst, ssem, rsem, device):
        copy = pltpu.make_async_remote_copy(
            src_ref=src, dst_ref=dst, send_sem=ssem, recv_sem=rsem,
            device_id=device, device_id_type=MESH,
        )
        copy.start()
        sends.append(copy)

    def wait_recv(ref, ssem, rsem, device):
        pltpu.make_async_remote_copy(
            src_ref=ref, dst_ref=ref, send_sem=ssem, recv_sem=rsem,
            device_id=device, device_id_type=MESH,
        ).wait_recv()

    def piece(d, core, chip_col):
        return xg.at[
            d - 1,
            pl.ds(pl.multiple_of(core * half, 32), half),
            pl.ds(pl.multiple_of(chip_col * q, 128), q),
        ]

    def share(d):
        wait_recv(piece(d, k, c), bx1s.at[d - 1], bx1r.at[d - 1], (s, j))
        mine = piece(d, k, c)
        send(mine, mine, bx2s.at[d - 1, 0], bx2r.at[d - 1, 0], (s, dev_x))
        send(mine, mine, bx2s.at[d - 1, 1], bx2r.at[d - 1, 1], (s, dev_y))
        send(mine, mine, bx2s.at[d - 1, 2], bx2r.at[d - 1, 2], (s, dev_d))

    def meet(d):
        for n, (col, dev) in enumerate(((c_x, dev_x), (c_y, dev_y), (c_d, dev_d))):
            wait_recv(piece(d, k, col), bx2s.at[d - 1, n], bx2r.at[d - 1, n], (s, dev))
        send(token_half(d, k), token_half(d, k), bx3s.at[d - 1], bx3r.at[d - 1], (s, sibling))

    def token_half(d, core):
        return xg.at[d - 1, pl.ds(pl.multiple_of(core * half, 32), half), :]

    def exchange(d):
        src = x_hbm.at[
            pl.ds(pl.multiple_of(k * half, 32), half),
            pl.ds(pl.multiple_of(seq_peer(d) * blk + c * q, 128), q),
        ]
        send(src, piece(d, k, c), bx1s.at[d - 1], bx1r.at[d - 1], (seq_peer(d), j))

    for d in order:
        exchange(d)

    proj = jnp.zeros((3 * DH, rows), F32)
    for i in range(LOAD_CHUNKS):
        cols = pl.ds(i * wide, wide)
        loads[2 * i].wait()
        loads[2 * i + 1].wait()
        proj = proj + mm_nt(w[:, cols], x[:, cols])
    q_t = (proj[:DH] * scale).astype(BF16)
    k_t = proj[DH : 2 * DH].astype(BF16)
    v_t = proj[2 * DH :].astype(BF16)
    for copy in smalls:
        copy.wait()
    o = o_ref[...]
    o_t = o.astype(F32).T.astype(BF16)
    q_r = q_t.astype(F32).T.astype(BF16)
    v_r = v_t.astype(F32).T.astype(BF16)

    rate = rate_ref[0]
    n_events = events_ref.shape[0]
    base = s * rows
    lane = lax.broadcasted_iota(jnp.int32, (1, rows), 1)

    def events_in(low, high):
        total = jnp.zeros(jnp.broadcast_shapes(jnp.shape(low), jnp.shape(high)), F32)
        for n in range(n_events):
            e = events_ref[n]
            total = total + jnp.where((e > low) & (e <= high), 1.0, 0.0)
        return total

    last = jnp.full((1, rows), rows - 1, jnp.int32) + base
    before = jnp.full((1, rows), -1, jnp.int32) + base
    here = lane + base
    head_w = jnp.exp(-(rate * (lane + 1).astype(F32) + DROP_LOGARITHM * events_in(before, here)))
    tail_w = jnp.exp(
        -(rate * (rows - 1 - lane).astype(F32) + DROP_LOGARITHM * events_in(here, last))
    )

    st[0, 0] = mm((k_t.astype(F32) * tail_w).astype(BF16), v_r).astype(BF16)
    st[1, 0] = mm((q_t.astype(F32) * head_w).astype(BF16), o).astype(BF16)
    for d in range(1, n_seq):
        earlier = jnp.where(seq_peer(d) < s, 1, 0)
        send(st.at[earlier, 0], st.at[0, d], sts.at[d - 1], str_.at[d - 1], (seq_peer(d), j))

    for d in first:
        share(d)

    t_idx = lax.broadcasted_iota(jnp.int32, (rows, rows), 0)
    s_idx = lax.broadcasted_iota(jnp.int32, (rows, rows), 1)
    decay = rate * (t_idx - s_idx).astype(F32) + DROP_LOGARITHM * events_in(
        s_idx + base, t_idx + base
    )
    weight = jnp.where(t_idx >= s_idx, jnp.exp(-jnp.maximum(decay, 0.0)), 0.0)
    scores = (mm(q_r, k_t) * weight).astype(BF16)
    dscores = (mm(o, v_t) * weight).astype(BF16)
    dq_t = mm_nt(k_t, dscores)
    dk_t = mm(q_t, dscores)
    dv_t = mm(o_t, scores)

    for d in rest:
        share(d)

    prefix = jnp.zeros((DH, DH), F32)
    suffix = jnp.zeros((DH, DH), F32)
    zero = jnp.zeros((1, DH), jnp.int32)
    for d in range(1, n_seq):
        wait_recv(st.at[0, d], sts.at[d - 1], str_.at[d - 1], (s, j))
        src = lax.rem(s + n_seq - d, n_seq)
        state = st[0, d].astype(F32)
        low = jnp.minimum(src, s)
        high = jnp.maximum(src, s)
        gap = rate * ((high - low - 1) * rows).astype(F32) + DROP_LOGARITHM * events_in(
            zero + ((low + 1) * rows - 1), zero + (high * rows - 1)
        )
        state = state * jnp.exp(-gap)
        is_fwd = (zero + src) < (zero + s)
        prefix = prefix + jnp.where(is_fwd, state, 0.0)
        suffix = suffix + jnp.where(is_fwd, 0.0, state)
    dq_t = dq_t + mm(prefix.astype(BF16), o_t) * head_w
    dk_t = dk_t + mm(suffix.astype(BF16), v_t) * tail_w
    dv_t = dv_t + mm(suffix.T.astype(BF16), k_t) * tail_w
    grads_t = jnp.concatenate([dq_t * scale, dk_t, dv_t], axis=0)
    gt[0] = grads_t.astype(BF16)
    g[...] = grads_t.T.astype(BF16)
    head, tail = 128, rows - 128
    low, high = grads_t[: 3 * DH // 2, head:], grads_t[3 * DH // 2 :, head:]
    gx[0, : 3 * DH] = grads_t[:, :head].astype(BF16)
    gx[0, 3 * DH :] = jnp.concatenate([low, high], axis=1).astype(BF16)
    for d in range(1, n_seq):
        send(gx.at[0], gx.at[d], gs.at[d - 1], gr.at[d - 1], (seq_peer(d), j))

    if not aligned:
        wb_copy.wait()

    def block_term(owner, put):
        if aligned:
            put(pl.ds(0, iblk), mm(g[...], w[:, pl.ds(pl.multiple_of(owner * iblk, 128), iblk)]))
        else:
            put(pl.ds(0, iblk), mm(g[...], wb[owner]))

    if nc == 4:
        chip_x, chip_y, chip_d = across(chip)
        chips = [chip_d, chip_x, chip_y, chip]
    else:
        chips = [lax.rem(chip + m, nc) for m in range(1, nc + 1)]
    for m in range(nc):
        def put(cols, value, m=m):
            ps[m, :, cols] = value.astype(BF16)
        block_term(2 * chips[m] + 1 - k, put)
        send(ps.at[m], rc.at[m], pss.at[m], psr.at[m], (s, sibling))

    def pair_sum(m, put):
        wait_recv(rc.at[m], pss.at[m], psr.at[m], (s, sibling))
        def put_sum(cols, value):
            put(cols, value + rc[m, :, cols].astype(F32))
        block_term(2 * chips[m] + k, put_sum)

    if nc == 4:
        to_x, to_y = (s, 2 * chip_x + k), (s, 2 * chip_y + k)
        top, bottom = pl.ds(0, half), pl.ds(half, half)
        targets = [
            (rt.at[0], to_x), (rt.at[1], to_y),
            (rd.at[0, top], to_x), (rd.at[1, bottom], to_y),
            (rd.at[0, bottom], to_x), (rd.at[1, top], to_y),
        ]

        def send_part(n):
            send(sd.at[n], targets[n][0], rds.at[n], rdr.at[n], targets[n][1])

        def wait_part(n):
            wait_recv(targets[n][0], rds.at[n], rdr.at[n], targets[n][1])

        for m, (a, b) in enumerate(((0, 1), (2, 4), (5, 3))):
            def put(cols, value, a=a, b=b):
                sd[a, :, cols] = value[:half].astype(BF16)
                sd[b, :, cols] = value[half:].astype(BF16)
            pair_sum(m, put)
            for n in (a, b):
                if n < 4:
                    send_part(n)
        for n, got in ((4, 1), (5, 0)):
            wait_part(got)
            sd[n] = (sd[n].astype(F32) + rt[got].astype(F32)).astype(BF16)
            send_part(n)
        arrivals = 2
    else:
        for m in range(nc - 1):
            def put(cols, value, m=m):
                sd[m, :, cols] = value.astype(BF16)
            pair_sum(m, put)
            send(sd.at[m], rd.at[m], rds.at[m], rdr.at[m], (s, 2 * chips[m] + k))
        arrivals = nc - 1
    for d in order:
        meet(d)

    def put(cols, value):
        own[:, cols] = value
    pair_sum(nc - 1, put)

    wstep = 256

    def arrived(d):
        wait_recv(gx.at[d], gs.at[d - 1], gr.at[d - 1], (s, j))
        gt[d, :, :head] = gx[d, : 3 * DH]
        packed = gx[d, 3 * DH :].astype(F32)
        gt[d, : 3 * DH // 2, head:] = packed[:, :tail].astype(BF16)
        gt[d, 3 * DH // 2 :, head:] = packed[:, tail:].astype(BF16)
        wait_recv(token_half(d, 1 - k), bx3s.at[d - 1], bx3r.at[d - 1], (s, sibling))

    for d in first:
        arrived(d)
    for i in range(blk // wstep):
        cols = pl.ds(i * wstep, wstep)
        total = mm(gt[0], x[:, pl.ds(pl.multiple_of(s * blk + i * wstep, 128), wstep)])
        for d in first:
            total = total + mm(gt[d], xg[d - 1, :, cols])
        acc[:, cols] = total
    for d in rest:
        arrived(d)
    square = jnp.zeros((8, wstep), F32)
    for i in range(blk // wstep):
        cols = pl.ds(i * wstep, wstep)
        total = acc[:, cols]
        for d in rest:
            total = total + mm(gt[d], xg[d - 1, :, cols])
        acc[:, cols] = total
        square = square + jnp.sum((total * total).reshape(3 * DH // 8, 8, wstep), axis=0)
    sqt[0] = square[:, :128] + square[:, 128:]
    if flat:
        for i, (a, b) in enumerate(offsets):
            to = (seq_peer(a), t_peer(b))
            send(sqt.at[0], sqt.at[i + 1], ts.at[i], tr.at[i], to)
    else:
        sqz[0] = sqt[0]
        for d in range(1, n_seq):
            send(sqz.at[0], sqz.at[d], zs.at[d - 1], zr.at[d - 1], (seq_peer(d), j))

    def finish():
        if nc == 4:
            for n in range(2, 6):
                wait_part(n)
        else:
            for m in range(arrivals):
                wait_recv(rd.at[m], rds.at[m], rdr.at[m], (s, j))
        total = own[...]
        for m in range(arrivals):
            total = total + rd[m].astype(F32)
        ig_ref[...] = total.astype(BF16)

    if flat:
        finish()
        peers = len(offsets)
    else:
        for d in range(1, n_seq):
            wait_recv(sqz.at[d], zs.at[d - 1], zr.at[d - 1], (s, j))
        total = sqz[0]
        for d in range(1, n_seq):
            total = total + sqz[d]
        sqt[0] = total
        for d in range(1, n_t):
            send(sqt.at[0], sqt.at[d], ts.at[d - 1], tr.at[d - 1], (s, t_peer(d)))
        finish()
        peers = n_t - 1
    for i in range(peers):
        wait_recv(sqt.at[i + 1], ts.at[i], tr.at[i], (s, j))
    total = sqt[0]
    for i in range(peers):
        total = total + sqt[i + 1]
    total = jnp.sum(jnp.sum(total, axis=1, keepdims=True), axis=0, keepdims=True)
    factor = jnp.minimum(1.0, CLIP_RMS * math.sqrt(entries) / jnp.sqrt(total + 1e-06))

    def scaled(i, carry):
        cols = pl.ds(pl.multiple_of(i * wstep, 128), wstep)
        wg_ref[:, cols] = (acc[:, cols] * factor).astype(BF16)
        return carry

    lax.fori_loop(0, blk // wstep, scaled, 0)
    for copy in sends:
        copy.wait_send()


def body(n_seq, n_t, layer_inputs, projection_matrices, result_sensitivity, rate, events):
    rows, width = layer_inputs.shape
    blk, iblk, nc = width // n_seq, width // n_t, n_t // 2
    aligned = iblk % 128 == 0
    w_t = projection_matrices.transpose(1, 2, 0).reshape(3 * DH, width)
    if aligned:
        w_b = result_sensitivity
    else:
        w_b = w_t.reshape(3 * DH, n_t, iblk).transpose(1, 0, 2)
    entries = width * 3 * DH * n_t
    flat = n_seq * n_t <= 64
    peers = n_seq * n_t - 1 if flat else n_t - 1
    dma = pltpu.SemaphoreType.DMA
    vmem = pl.BlockSpec(memory_space=pltpu.VMEM)
    z = n_seq - 1
    input_t, weight_t = pl.pallas_call(
        functools.partial(kernel, n_seq, n_t, entries, aligned, flat),
        out_shape=(
            pltpu.VMEM((rows, iblk), BF16),
            pltpu.VMEM((3 * DH, blk), BF16),
        ),
        in_specs=[pl.BlockSpec(memory_space=pltpu.HBM)] * 6,
        out_specs=(vmem, vmem),
        scratch_shapes=[
            pltpu.VMEM((rows, width), BF16),
            pltpu.VMEM((3 * DH, width), BF16),
            pltpu.VMEM((8, 128) if aligned else w_b.shape, BF16),
            pltpu.VMEM(result_sensitivity.shape, BF16),
            pltpu.SMEM(rate.shape, F32),
            pltpu.SMEM(events.shape, jnp.int32),
            pltpu.VMEM((z, rows, blk), BF16),
            pltpu.VMEM((rows, 3 * DH), BF16),
            pltpu.VMEM((n_seq, 9 * DH // 2, 128), BF16),
            pltpu.VMEM((n_seq, 3 * DH, rows), BF16),
            pltpu.VMEM((2, n_seq, DH, DH), BF16),
            pltpu.VMEM((nc, rows, iblk), BF16),
            pltpu.VMEM((nc, rows, iblk), BF16),
            pltpu.VMEM((6, rows // 2, iblk) if nc == 4 else (nc - 1, rows, iblk), BF16),
            pltpu.VMEM((2, rows // 2, iblk), BF16),
            pltpu.VMEM((2 if nc == 4 else nc - 1, rows, iblk), BF16),
            pltpu.VMEM((rows, iblk), F32),
            pltpu.VMEM((3 * DH, blk), F32),
            pltpu.VMEM((n_seq, 8, 128), F32),
            pltpu.VMEM((peers + 1, 8, 128), F32),
            dma((2 * LOAD_CHUNKS + 1,)), dma((3,)),
            dma((z,)), dma((z,)),
            dma((z, 3)), dma((z, 3)),
            dma((z,)), dma((z,)),
            dma((z,)), dma((z,)),
            dma((z,)), dma((z,)),
            dma((nc,)), dma((nc,)),
            dma((6 if nc == 4 else nc - 1,)), dma((6 if nc == 4 else nc - 1,)),
            dma((z,)), dma((z,)),
            dma((peers,)), dma((peers,)),
        ],
        compiler_params=pltpu.CompilerParams(
            collective_id=0, has_side_effects=True, vmem_limit_bytes=60 * 1024 * 1024
        ),
    )(layer_inputs, w_t, w_b, result_sensitivity, rate, events)
    weight_grad = weight_t.reshape(3, DH, blk).transpose(2, 0, 1)
    return input_t.T, weight_grad


def solution(mesh):
    return jax.shard_map(
        functools.partial(body, mesh.shape["seq"], mesh.shape["tensor"]),
        mesh=mesh,
        in_specs=(P("seq", None), P(None, None, "tensor"), P("seq", "tensor"), P("tensor"), P()),
        out_specs=(P("tensor", "seq"), P("seq", None, "tensor")),
        check_vma=False,
    )
```

```python
import functools
import math

import jax
import jax.numpy as jnp
from jax import lax
from jax.experimental import pallas as pl
from jax.experimental.pallas import tpu as pltpu
from jax.sharding import PartitionSpec as P

DH = 96
DROP_LOGARITHM = 0.3
CLIP_RMS = 0.5
MESH = pl.DeviceIdType.MESH
F32 = jnp.float32
BF16 = jnp.bfloat16
LOAD_CHUNKS = 4
WRITE_CHUNKS = 3


def mm(a, b):
    return jnp.dot(a, b, preferred_element_type=F32)


def mm_nt(a, b):
    return lax.dot_general(a, b, (((1,), (1,)), ((), ())), preferred_element_type=F32)


def kernel(
    n_seq, n_t, entries, aligned, flat,
    x_hbm, w_hbm, wb_hbm, o_hbm, rate_hbm, events_hbm,
    ig_ref, acc, factor_ref,
    x, w, wb, o_ref, rate_ref, events_ref,
    xg, g, gx, gt, st, ps, rc, sd, rt, rd, own, sqz, sqt,
    load_sem, small_sem, bx1s, bx1r, bx2s, bx2r, bx3s, bx3r, sts, str_, gs, gr,
    pss, psr, rds, rdr, zs, zr, ts, tr,
):
    rows, width = x_hbm.shape
    blk = width // n_seq
    iblk = width // n_t
    scale = DH ** (-0.5)
    s = lax.axis_index("seq")
    j = lax.axis_index("tensor")
    nc = n_t // 2
    k = lax.rem(j, 2)
    chip = j // 2
    sibling = j + 1 - 2 * k
    group = (j // 8) * 8
    c = lax.rem(j, 8) // 2
    q = blk // 4
    half = rows // 2
    order = sorted(range(1, n_seq), key=lambda d: min(d, n_seq - d))
    first, rest = order[: max(1, n_seq // 2)], order[max(1, n_seq // 2) :]

    def across(n):
        a, b = lax.rem(n, 2), lax.rem(n // 2, 2)
        return n + 1 - 2 * a, n + 2 - 4 * b, n + 3 - 2 * a - 4 * b

    c_x, c_y, c_d = across(c)
    dev_x, dev_y, dev_d = group + 2 * c_x + k, group + 2 * c_y + k, group + 2 * c_d + k

    wide = width // LOAD_CHUNKS
    loads = []
    for i in range(LOAD_CHUNKS):
        cols = pl.ds(i * wide, wide)
        for n, (src, dst) in enumerate(((x_hbm, x), (w_hbm, w))):
            copy = pltpu.make_async_copy(src.at[:, cols], dst.at[:, cols], load_sem.at[2 * i + n])
            copy.start()
            loads.append(copy)
    smalls = []
    for n, (src, dst) in enumerate(((o_hbm, o_ref), (rate_hbm, rate_ref), (events_hbm, events_ref))):
        copy = pltpu.make_async_copy(src, dst, small_sem.at[n])
        copy.start()
        smalls.append(copy)
    if not aligned:
        wb_copy = pltpu.make_async_copy(wb_hbm, wb, load_sem.at[2 * LOAD_CHUNKS])
        wb_copy.start()

    def seq_peer(d):
        return lax.rem(s + d, n_seq)

    def t_peer(d):
        return lax.rem(j + d, n_t)

    offsets = [(a, b) for a in range(n_seq) for b in range(n_t) if (flat or a * b == 0) and a + b]
    barrier = pltpu.get_barrier_semaphore()
    for a, b in offsets:
        pl.semaphore_signal(barrier, inc=1, device_id=(seq_peer(a), t_peer(b)), device_id_type=MESH)
    pl.semaphore_wait(barrier, len(offsets))

    sends = []

    def send(src, dst, ssem, rsem, device):
        copy = pltpu.make_async_remote_copy(
            src_ref=src, dst_ref=dst, send_sem=ssem, recv_sem=rsem,
            device_id=device, device_id_type=MESH,
        )
        copy.start()
        sends.append(copy)

    def wait_recv(ref, ssem, rsem, device):
        pltpu.make_async_remote_copy(
            src_ref=ref, dst_ref=ref, send_sem=ssem, recv_sem=rsem,
            device_id=device, device_id_type=MESH,
        ).wait_recv()

    def piece(d, core, chip_col):
        return xg.at[
            d - 1,
            pl.ds(pl.multiple_of(core * half, 32), half),
            pl.ds(pl.multiple_of(chip_col * q, 128), q),
        ]

    def share(d):
        wait_recv(piece(d, k, c), bx1s.at[d - 1], bx1r.at[d - 1], (s, j))
        mine = piece(d, k, c)
        send(mine, mine, bx2s.at[d - 1, 0], bx2r.at[d - 1, 0], (s, dev_x))
        send(mine, mine, bx2s.at[d - 1, 1], bx2r.at[d - 1, 1], (s, dev_y))
        send(mine, mine, bx2s.at[d - 1, 2], bx2r.at[d - 1, 2], (s, dev_d))

    def meet(d):
        for n, (col, dev) in enumerate(((c_x, dev_x), (c_y, dev_y), (c_d, dev_d))):
            wait_recv(piece(d, k, col), bx2s.at[d - 1, n], bx2r.at[d - 1, n], (s, dev))
        send(token_half(d, k), token_half(d, k), bx3s.at[d - 1], bx3r.at[d - 1], (s, sibling))

    def token_half(d, core):
        return xg.at[d - 1, pl.ds(pl.multiple_of(core * half, 32), half), :]

    def exchange(d):
        src = x_hbm.at[
            pl.ds(pl.multiple_of(k * half, 32), half),
            pl.ds(pl.multiple_of(seq_peer(d) * blk + c * q, 128), q),
        ]
        send(src, piece(d, k, c), bx1s.at[d - 1], bx1r.at[d - 1], (seq_peer(d), j))

    for d in first:
        exchange(d)

    proj = jnp.zeros((3 * DH, rows), F32)
    for i in range(LOAD_CHUNKS):
        cols = pl.ds(i * wide, wide)
        loads[2 * i].wait()
        loads[2 * i + 1].wait()
        proj = proj + mm_nt(w[:, cols], x[:, cols])
    q_t = (proj[:DH] * scale).astype(BF16)
    k_t = proj[DH : 2 * DH].astype(BF16)
    v_t = proj[2 * DH :].astype(BF16)
    for copy in smalls:
        copy.wait()
    o = o_ref[...]
    o_t = o.astype(F32).T.astype(BF16)
    q_r = q_t.astype(F32).T.astype(BF16)
    v_r = v_t.astype(F32).T.astype(BF16)

    rate = rate_ref[0]
    n_events = events_ref.shape[0]
    base = s * rows
    lane = lax.broadcasted_iota(jnp.int32, (1, rows), 1)

    def events_in(low, high):
        total = jnp.zeros(jnp.broadcast_shapes(jnp.shape(low), jnp.shape(high)), F32)
        for n in range(n_events):
            e = events_ref[n]
            total = total + jnp.where((e > low) & (e <= high), 1.0, 0.0)
        return total

    last = jnp.full((1, rows), rows - 1, jnp.int32) + base
    before = jnp.full((1, rows), -1, jnp.int32) + base
    here = lane + base
    head_w = jnp.exp(-(rate * (lane + 1).astype(F32) + DROP_LOGARITHM * events_in(before, here)))
    tail_w = jnp.exp(
        -(rate * (rows - 1 - lane).astype(F32) + DROP_LOGARITHM * events_in(here, last))
    )

    st[0, 0] = mm((k_t.astype(F32) * tail_w).astype(BF16), v_r).astype(BF16)
    st[1, 0] = mm((q_t.astype(F32) * head_w).astype(BF16), o).astype(BF16)
    for d in range(1, n_seq):
        earlier = jnp.where(seq_peer(d) < s, 1, 0)
        send(st.at[earlier, 0], st.at[0, d], sts.at[d - 1], str_.at[d - 1], (seq_peer(d), j))

    for d in rest:
        exchange(d)

    t_idx = lax.broadcasted_iota(jnp.int32, (rows, rows), 0)
    s_idx = lax.broadcasted_iota(jnp.int32, (rows, rows), 1)
    decay = rate * (t_idx - s_idx).astype(F32) + DROP_LOGARITHM * events_in(
        s_idx + base, t_idx + base
    )
    weight = jnp.where(t_idx >= s_idx, jnp.exp(-jnp.maximum(decay, 0.0)), 0.0)
    scores = (mm(q_r, k_t) * weight).astype(BF16)
    dscores = (mm(o, v_t) * weight).astype(BF16)
    dq_t = mm_nt(k_t, dscores)
    dk_t = mm(q_t, dscores)
    dv_t = mm(o_t, scores)

    for d in first:
        share(d)

    prefix = jnp.zeros((DH, DH), F32)
    suffix = jnp.zeros((DH, DH), F32)
    zero = jnp.zeros((1, DH), jnp.int32)
    for d in range(1, n_seq):
        wait_recv(st.at[0, d], sts.at[d - 1], str_.at[d - 1], (s, j))
        src = lax.rem(s + n_seq - d, n_seq)
        state = st[0, d].astype(F32)
        low = jnp.minimum(src, s)
        high = jnp.maximum(src, s)
        gap = rate * ((high - low - 1) * rows).astype(F32) + DROP_LOGARITHM * events_in(
            zero + ((low + 1) * rows - 1), zero + (high * rows - 1)
        )
        state = state * jnp.exp(-gap)
        is_fwd = (zero + src) < (zero + s)
        prefix = prefix + jnp.where(is_fwd, state, 0.0)
        suffix = suffix + jnp.where(is_fwd, 0.0, state)
    dq_t = dq_t + mm(prefix.astype(BF16), o_t) * head_w
    dk_t = dk_t + mm(suffix.astype(BF16), v_t) * tail_w
    dv_t = dv_t + mm(suffix.T.astype(BF16), k_t) * tail_w
    grads_t = jnp.concatenate([dq_t * scale, dk_t, dv_t], axis=0)
    gt[0] = grads_t.astype(BF16)
    g[...] = grads_t.T.astype(BF16)
    head, tail = 128, rows - 128
    low, high = grads_t[: 3 * DH // 2, head:], grads_t[3 * DH // 2 :, head:]
    gx[0, : 3 * DH] = grads_t[:, :head].astype(BF16)
    gx[0, 3 * DH :] = jnp.concatenate([low, high], axis=1).astype(BF16)
    for d in range(1, n_seq):
        send(gx.at[0], gx.at[d], gs.at[d - 1], gr.at[d - 1], (seq_peer(d), j))

    if not aligned:
        wb_copy.wait()

    def block_term(owner, put):
        if aligned:
            put(pl.ds(0, iblk), mm(g[...], w[:, pl.ds(pl.multiple_of(owner * iblk, 128), iblk)]))
        else:
            put(pl.ds(0, iblk), mm(g[...], wb[owner]))

    if nc == 4:
        chip_x, chip_y, chip_d = across(chip)
        chips = [chip_d, chip_x, chip_y, chip]
    else:
        chips = [lax.rem(chip + m, nc) for m in range(1, nc + 1)]
    for m in range(nc):
        def put(cols, value, m=m):
            ps[m, :, cols] = value.astype(BF16)
        block_term(2 * chips[m] + 1 - k, put)
        send(ps.at[m], rc.at[m], pss.at[m], psr.at[m], (s, sibling))
    for d in rest:
        share(d)

    def pair_sum(m, put):
        wait_recv(rc.at[m], pss.at[m], psr.at[m], (s, sibling))
        def put_sum(cols, value):
            put(cols, value + rc[m, :, cols].astype(F32))
        block_term(2 * chips[m] + k, put_sum)

    wstep = 256

    def own_work():
        def put(cols, value):
            own[:, cols] = value
        pair_sum(nc - 1, put)
        for i in range(blk // wstep):
            cols = pl.ds(pl.multiple_of(s * blk + i * wstep, 128), wstep)
            acc[:, pl.ds(i * wstep, wstep)] = mm(gt[0], x[:, cols])

    if nc == 4:
        to_x, to_y = (s, 2 * chip_x + k), (s, 2 * chip_y + k)
        top, bottom = pl.ds(0, half), pl.ds(half, half)
        targets = [
            (rt.at[0], to_x), (rt.at[1], to_y),
            (rd.at[0, top], to_x), (rd.at[1, bottom], to_y),
            (rd.at[0, bottom], to_x), (rd.at[1, top], to_y),
        ]

        def send_part(n):
            send(sd.at[n], targets[n][0], rds.at[n], rdr.at[n], targets[n][1])

        def wait_part(n):
            wait_recv(targets[n][0], rds.at[n], rdr.at[n], targets[n][1])

        for m, (a, b) in enumerate(((0, 1), (2, 4), (5, 3))):
            def put(cols, value, a=a, b=b):
                sd[a, :, cols] = value[:half].astype(BF16)
                sd[b, :, cols] = value[half:].astype(BF16)
            pair_sum(m, put)
            for n in (a, b):
                if n < 4:
                    send_part(n)
        own_work()
        for n, got in ((4, 1), (5, 0)):
            wait_part(got)
            sd[n] = (sd[n].astype(F32) + rt[got].astype(F32)).astype(BF16)
            send_part(n)
        arrivals = 2
    else:
        for m in range(nc - 1):
            def put(cols, value, m=m):
                sd[m, :, cols] = value.astype(BF16)
            pair_sum(m, put)
            send(sd.at[m], rd.at[m], rds.at[m], rdr.at[m], (s, 2 * chips[m] + k))
        own_work()
        arrivals = nc - 1
    for d in order:
        meet(d)


    def arrived(d):
        wait_recv(gx.at[d], gs.at[d - 1], gr.at[d - 1], (s, j))
        gt[d, :, :head] = gx[d, : 3 * DH]
        packed = gx[d, 3 * DH :].astype(F32)
        gt[d, : 3 * DH // 2, head:] = packed[:, :tail].astype(BF16)
        gt[d, 3 * DH // 2 :, head:] = packed[:, tail:].astype(BF16)
        wait_recv(token_half(d, 1 - k), bx3s.at[d - 1], bx3r.at[d - 1], (s, sibling))

    for d in first:
        arrived(d)
    for i in range(blk // wstep):
        cols = pl.ds(i * wstep, wstep)
        total = acc[:, cols]
        for d in first:
            total = total + mm(gt[d], xg[d - 1, :, cols])
        acc[:, cols] = total
    for d in rest:
        arrived(d)
    square = jnp.zeros((8, wstep), F32)
    for i in range(blk // wstep):
        cols = pl.ds(i * wstep, wstep)
        total = acc[:, cols]
        for d in rest:
            total = total + mm(gt[d], xg[d - 1, :, cols])
        acc[:, cols] = total
        square = square + jnp.sum((total * total).reshape(3 * DH // 8, 8, wstep), axis=0)
    sqt[0] = square[:, :128] + square[:, 128:]
    if flat:
        for i, (a, b) in enumerate(offsets):
            to = (seq_peer(a), t_peer(b))
            send(sqt.at[0], sqt.at[i + 1], ts.at[i], tr.at[i], to)
    else:
        sqz[0] = sqt[0]
        for d in range(1, n_seq):
            send(sqz.at[0], sqz.at[d], zs.at[d - 1], zr.at[d - 1], (seq_peer(d), j))

    def finish():
        if nc == 4:
            for n in range(2, 6):
                wait_part(n)
        else:
            for m in range(arrivals):
                wait_recv(rd.at[m], rds.at[m], rdr.at[m], (s, j))
        total = own[...]
        for m in range(arrivals):
            total = total + rd[m].astype(F32)
        ig_ref[...] = total.astype(BF16)

    if flat:
        finish()
        peers = len(offsets)
    else:
        for d in range(1, n_seq):
            wait_recv(sqz.at[d], zs.at[d - 1], zr.at[d - 1], (s, j))
        total = sqz[0]
        for d in range(1, n_seq):
            total = total + sqz[d]
        sqt[0] = total
        for d in range(1, n_t):
            send(sqt.at[0], sqt.at[d], ts.at[d - 1], tr.at[d - 1], (s, t_peer(d)))
        finish()
        peers = n_t - 1
    for i in range(peers):
        wait_recv(sqt.at[i + 1], ts.at[i], tr.at[i], (s, j))
    total = sqt[0]
    for i in range(peers):
        total = total + sqt[i + 1]
    total = jnp.sum(jnp.sum(total, axis=1, keepdims=True), axis=0, keepdims=True)
    factor = jnp.minimum(1.0, CLIP_RMS * math.sqrt(entries) / jnp.sqrt(total + 1e-06))

    factor_ref[...] = jnp.broadcast_to(factor, (8, 128))
    for copy in sends:
        copy.wait_send()


def write(input_sum, summed, factor_ref, ig_hbm, wg_hbm, scaled, sems):
    copies = [pltpu.make_async_copy(input_sum, ig_hbm, sems.at[0])]
    copies[0].start()
    factor = factor_ref[:1, :1]
    tall = summed.shape[0] // WRITE_CHUNKS
    for i in range(WRITE_CHUNKS):
        part = pl.ds(i * tall, tall)
        scaled[part, :] = (summed[part, :] * factor).astype(BF16)
        copy = pltpu.make_async_copy(scaled.at[part], wg_hbm.at[part], sems.at[i + 1])
        copy.start()
        copies.append(copy)
    for copy in copies:
        copy.wait()


def body(n_seq, n_t, layer_inputs, projection_matrices, result_sensitivity, rate, events):
    rows, width = layer_inputs.shape
    blk, iblk, nc = width // n_seq, width // n_t, n_t // 2
    aligned = iblk % 128 == 0
    w_t = projection_matrices.transpose(1, 2, 0).reshape(3 * DH, width)
    if aligned:
        w_b = result_sensitivity
    else:
        w_b = w_t.reshape(3 * DH, n_t, iblk).transpose(1, 0, 2)
    entries = width * 3 * DH * n_t
    flat = n_seq * n_t <= 64
    peers = n_seq * n_t - 1 if flat else n_t - 1
    dma = pltpu.SemaphoreType.DMA
    vmem = pl.BlockSpec(memory_space=pltpu.VMEM)
    z = n_seq - 1
    input_sum, summed, factor = pl.pallas_call(
        functools.partial(kernel, n_seq, n_t, entries, aligned, flat),
        out_shape=(
            pltpu.VMEM((rows, iblk), BF16),
            pltpu.VMEM((3 * DH, blk), F32),
            pltpu.VMEM((8, 128), F32),
        ),
        in_specs=[pl.BlockSpec(memory_space=pltpu.HBM)] * 6,
        out_specs=(vmem, vmem, vmem),
        scratch_shapes=[
            pltpu.VMEM((rows, width), BF16),
            pltpu.VMEM((3 * DH, width), BF16),
            pltpu.VMEM((8, 128) if aligned else w_b.shape, BF16),
            pltpu.VMEM(result_sensitivity.shape, BF16),
            pltpu.SMEM(rate.shape, F32),
            pltpu.SMEM(events.shape, jnp.int32),
            pltpu.VMEM((z, rows, blk), BF16),
            pltpu.VMEM((rows, 3 * DH), BF16),
            pltpu.VMEM((n_seq, 9 * DH // 2, 128), BF16),
            pltpu.VMEM((n_seq, 3 * DH, rows), BF16),
            pltpu.VMEM((2, n_seq, DH, DH), BF16),
            pltpu.VMEM((nc, rows, iblk), BF16),
            pltpu.VMEM((nc, rows, iblk), BF16),
            pltpu.VMEM((6, rows // 2, iblk) if nc == 4 else (nc - 1, rows, iblk), BF16),
            pltpu.VMEM((2, rows // 2, iblk), BF16),
            pltpu.VMEM((2 if nc == 4 else nc - 1, rows, iblk), BF16),
            pltpu.VMEM((rows, iblk), F32),
            pltpu.VMEM((n_seq, 8, 128), F32),
            pltpu.VMEM((peers + 1, 8, 128), F32),
            dma((2 * LOAD_CHUNKS + 1,)), dma((3,)),
            dma((z,)), dma((z,)),
            dma((z, 3)), dma((z, 3)),
            dma((z,)), dma((z,)),
            dma((z,)), dma((z,)),
            dma((z,)), dma((z,)),
            dma((nc,)), dma((nc,)),
            dma((6 if nc == 4 else nc - 1,)), dma((6 if nc == 4 else nc - 1,)),
            dma((z,)), dma((z,)),
            dma((peers,)), dma((peers,)),
        ],
        compiler_params=pltpu.CompilerParams(
            collective_id=0, has_side_effects=True, vmem_limit_bytes=56 * 1024 * 1024
        ),
    )(layer_inputs, w_t, w_b, result_sensitivity, rate, events)
    whole = pl.BlockSpec(memory_space=pl.ANY)
    input_t, weight_t = pl.pallas_call(
        write,
        out_shape=(
            jax.ShapeDtypeStruct((rows, iblk), BF16),
            jax.ShapeDtypeStruct((3 * DH, blk), BF16),
        ),
        in_specs=[vmem] * 3,
        out_specs=(whole, whole),
        scratch_shapes=[
            pltpu.VMEM((3 * DH, blk), BF16),
            dma((WRITE_CHUNKS + 1,)),
        ],
        compiler_params=pltpu.CompilerParams(vmem_limit_bytes=16 * 1024 * 1024),
    )(input_sum, summed, factor)
    weight_grad = weight_t.reshape(3, DH, blk).transpose(2, 0, 1)
    return input_t.T, weight_grad


def solution(mesh):
    return jax.shard_map(
        functools.partial(body, mesh.shape["seq"], mesh.shape["tensor"]),
        mesh=mesh,
        in_specs=(P("seq", None), P(None, None, "tensor"), P("seq", "tensor"), P("tensor"), P()),
        out_specs=(P("tensor", "seq"), P("seq", None, "tensor")),
        check_vma=False,
    )
```

```python
import functools
import math

import jax
import jax.numpy as jnp
from jax import lax
from jax.experimental import pallas as pl
from jax.experimental.pallas import tpu as pltpu
from jax.sharding import PartitionSpec as P

DH = 96
DROP_LOGARITHM = 0.3
CLIP_RMS = 0.5
MESH = pl.DeviceIdType.MESH
F32 = jnp.float32
BF16 = jnp.bfloat16
LOAD_CHUNKS = 4
WRITE_CHUNKS = 3


def mm(a, b):
    return jnp.dot(a, b, preferred_element_type=F32)


def mm_nt(a, b):
    return lax.dot_general(a, b, (((1,), (1,)), ((), ())), preferred_element_type=F32)


def kernel(
    n_seq, n_t, entries, aligned, flat,
    x_hbm, w_hbm, wb_hbm, o_hbm, rate_hbm, events_hbm,
    ig_ref, acc, factor_ref,
    x, w, wb, o_ref, rate_ref, events_ref,
    xg, g, gx, gt, st, ps, rc, sd, rt, rd, own, sqz, sqt,
    load_sem, small_sem, bx1s, bx1r, bx2s, bx2r, bx3s, bx3r, sts, str_, gs, gr,
    pss, psr, rds, rdr, zs, zr, ts, tr,
):
    rows, width = x_hbm.shape
    blk = width // n_seq
    iblk = width // n_t
    scale = DH ** (-0.5)
    s = lax.axis_index("seq")
    j = lax.axis_index("tensor")
    nc = n_t // 2
    k = lax.rem(j, 2)
    chip = j // 2
    sibling = j + 1 - 2 * k
    group = (j // 8) * 8
    c = lax.rem(j, 8) // 2
    q = blk // 4
    half = rows // 2
    order = sorted(range(1, n_seq), key=lambda d: min(d, n_seq - d))
    first, rest = order[: max(1, n_seq // 2)], order[max(1, n_seq // 2) :]

    def across(n):
        a, b = lax.rem(n, 2), lax.rem(n // 2, 2)
        return n + 1 - 2 * a, n + 2 - 4 * b, n + 3 - 2 * a - 4 * b

    c_x, c_y, c_d = across(c)
    dev_x, dev_y, dev_d = group + 2 * c_x + k, group + 2 * c_y + k, group + 2 * c_d + k

    wide = width // LOAD_CHUNKS
    loads = []
    for i in range(LOAD_CHUNKS):
        cols = pl.ds(i * wide, wide)
        for n, (src, dst) in enumerate(((x_hbm, x), (w_hbm, w))):
            copy = pltpu.make_async_copy(src.at[:, cols], dst.at[:, cols], load_sem.at[2 * i + n])
            copy.start()
            loads.append(copy)
    smalls = []
    for n, (src, dst) in enumerate(((o_hbm, o_ref), (rate_hbm, rate_ref), (events_hbm, events_ref))):
        copy = pltpu.make_async_copy(src, dst, small_sem.at[n])
        copy.start()
        smalls.append(copy)
    if not aligned:
        wb_copy = pltpu.make_async_copy(wb_hbm, wb, load_sem.at[2 * LOAD_CHUNKS])
        wb_copy.start()

    def seq_peer(d):
        return lax.rem(s + d, n_seq)

    def t_peer(d):
        return lax.rem(j + d, n_t)

    offsets = [(a, b) for a in range(n_seq) for b in range(n_t) if (flat or a * b == 0) and a + b]
    barrier = pltpu.get_barrier_semaphore()
    for a, b in offsets:
        pl.semaphore_signal(barrier, inc=1, device_id=(seq_peer(a), t_peer(b)), device_id_type=MESH)
    pl.semaphore_wait(barrier, len(offsets))

    sends = []

    def send(src, dst, ssem, rsem, device):
        copy = pltpu.make_async_remote_copy(
            src_ref=src, dst_ref=dst, send_sem=ssem, recv_sem=rsem,
            device_id=device, device_id_type=MESH,
        )
        copy.start()
        sends.append(copy)

    def wait_recv(ref, ssem, rsem, device):
        pltpu.make_async_remote_copy(
            src_ref=ref, dst_ref=ref, send_sem=ssem, recv_sem=rsem,
            device_id=device, device_id_type=MESH,
        ).wait_recv()

    def piece(d, core, chip_col):
        return xg.at[
            d - 1,
            pl.ds(pl.multiple_of(core * half, 32), half),
            pl.ds(pl.multiple_of(chip_col * q, 128), q),
        ]

    def share(d):
        wait_recv(piece(d, k, c), bx1s.at[d - 1], bx1r.at[d - 1], (s, j))
        mine = piece(d, k, c)
        send(mine, mine, bx2s.at[d - 1, 2], bx2r.at[d - 1, 2], (s, dev_d))
        send(mine, mine, bx2s.at[d - 1, 0], bx2r.at[d - 1, 0], (s, dev_x))
        send(mine, mine, bx2s.at[d - 1, 1], bx2r.at[d - 1, 1], (s, dev_y))

    def meet(d):
        for n, (col, dev) in enumerate(((c_x, dev_x), (c_y, dev_y), (c_d, dev_d))):
            wait_recv(piece(d, k, col), bx2s.at[d - 1, n], bx2r.at[d - 1, n], (s, dev))
        send(token_half(d, k), token_half(d, k), bx3s.at[d - 1], bx3r.at[d - 1], (s, sibling))

    def token_half(d, core):
        return xg.at[d - 1, pl.ds(pl.multiple_of(core * half, 32), half), :]

    def exchange(d):
        src = x_hbm.at[
            pl.ds(pl.multiple_of(k * half, 32), half),
            pl.ds(pl.multiple_of(seq_peer(d) * blk + c * q, 128), q),
        ]
        send(src, piece(d, k, c), bx1s.at[d - 1], bx1r.at[d - 1], (seq_peer(d), j))

    for d in order:
        exchange(d)

    proj = jnp.zeros((3 * DH, rows), F32)
    for i in range(LOAD_CHUNKS):
        cols = pl.ds(i * wide, wide)
        loads[2 * i].wait()
        loads[2 * i + 1].wait()
        proj = proj + mm_nt(w[:, cols], x[:, cols])
    q_t = (proj[:DH] * scale).astype(BF16)
    k_t = proj[DH : 2 * DH].astype(BF16)
    v_t = proj[2 * DH :].astype(BF16)
    for copy in smalls:
        copy.wait()
    o = o_ref[...]
    o_t = o.astype(F32).T.astype(BF16)
    q_r = q_t.astype(F32).T.astype(BF16)
    v_r = v_t.astype(F32).T.astype(BF16)

    rate = rate_ref[0]
    n_events = events_ref.shape[0]
    base = s * rows
    lane = lax.broadcasted_iota(jnp.int32, (1, rows), 1)

    def events_in(low, high):
        total = jnp.zeros(jnp.broadcast_shapes(jnp.shape(low), jnp.shape(high)), F32)
        for n in range(n_events):
            e = events_ref[n]
            total = total + jnp.where((e > low) & (e <= high), 1.0, 0.0)
        return total

    last = jnp.full((1, rows), rows - 1, jnp.int32) + base
    before = jnp.full((1, rows), -1, jnp.int32) + base
    here = lane + base
    head_w = jnp.exp(-(rate * (lane + 1).astype(F32) + DROP_LOGARITHM * events_in(before, here)))
    tail_w = jnp.exp(
        -(rate * (rows - 1 - lane).astype(F32) + DROP_LOGARITHM * events_in(here, last))
    )

    st[0, 0] = mm((k_t.astype(F32) * tail_w).astype(BF16), v_r).astype(BF16)
    st[1, 0] = mm((q_t.astype(F32) * head_w).astype(BF16), o).astype(BF16)
    for d in range(1, n_seq):
        earlier = jnp.where(seq_peer(d) < s, 1, 0)
        send(st.at[earlier, 0], st.at[0, d], sts.at[d - 1], str_.at[d - 1], (seq_peer(d), j))

    for d in first:
        share(d)

    t_idx = lax.broadcasted_iota(jnp.int32, (rows, rows), 0)
    s_idx = lax.broadcasted_iota(jnp.int32, (rows, rows), 1)
    decay = rate * (t_idx - s_idx).astype(F32) + DROP_LOGARITHM * events_in(
        s_idx + base, t_idx + base
    )
    weight = jnp.where(t_idx >= s_idx, jnp.exp(-jnp.maximum(decay, 0.0)), 0.0)
    scores = (mm(q_r, k_t) * weight).astype(BF16)
    dscores = (mm(o, v_t) * weight).astype(BF16)
    dq_t = mm_nt(k_t, dscores)
    dk_t = mm(q_t, dscores)
    dv_t = mm(o_t, scores)

    for d in rest:
        share(d)

    prefix = jnp.zeros((DH, DH), F32)
    suffix = jnp.zeros((DH, DH), F32)
    zero = jnp.zeros((1, DH), jnp.int32)
    for d in range(1, n_seq):
        wait_recv(st.at[0, d], sts.at[d - 1], str_.at[d - 1], (s, j))
        src = lax.rem(s + n_seq - d, n_seq)
        state = st[0, d].astype(F32)
        low = jnp.minimum(src, s)
        high = jnp.maximum(src, s)
        gap = rate * ((high - low - 1) * rows).astype(F32) + DROP_LOGARITHM * events_in(
            zero + ((low + 1) * rows - 1), zero + (high * rows - 1)
        )
        state = state * jnp.exp(-gap)
        is_fwd = (zero + src) < (zero + s)
        prefix = prefix + jnp.where(is_fwd, state, 0.0)
        suffix = suffix + jnp.where(is_fwd, 0.0, state)
    dq_t = dq_t + mm(prefix.astype(BF16), o_t) * head_w
    dk_t = dk_t + mm(suffix.astype(BF16), v_t) * tail_w
    dv_t = dv_t + mm(suffix.T.astype(BF16), k_t) * tail_w
    grads_t = jnp.concatenate([dq_t * scale, dk_t, dv_t], axis=0)
    gt[0] = grads_t.astype(BF16)
    g[...] = grads_t.T.astype(BF16)
    head, tail = 128, rows - 128
    low, high = grads_t[: 3 * DH // 2, head:], grads_t[3 * DH // 2 :, head:]
    gx[0, : 3 * DH] = grads_t[:, :head].astype(BF16)
    gx[0, 3 * DH :] = jnp.concatenate([low, high], axis=1).astype(BF16)
    for d in range(1, n_seq):
        send(gx.at[0], gx.at[d], gs.at[d - 1], gr.at[d - 1], (seq_peer(d), j))

    if not aligned:
        wb_copy.wait()

    def block_term(owner, put):
        if aligned:
            put(pl.ds(0, iblk), mm(g[...], w[:, pl.ds(pl.multiple_of(owner * iblk, 128), iblk)]))
        else:
            put(pl.ds(0, iblk), mm(g[...], wb[owner]))

    if nc == 4:
        chip_x, chip_y, chip_d = across(chip)
        chips = [chip_d, chip_x, chip_y, chip]
    else:
        chips = [lax.rem(chip + m, nc) for m in range(1, nc + 1)]
    for m in range(nc):
        def put(cols, value, m=m):
            ps[m, :, cols] = value.astype(BF16)
        block_term(2 * chips[m] + 1 - k, put)
        send(ps.at[m], rc.at[m], pss.at[m], psr.at[m], (s, sibling))

    def pair_sum(m, put):
        wait_recv(rc.at[m], pss.at[m], psr.at[m], (s, sibling))
        def put_sum(cols, value):
            put(cols, value + rc[m, :, cols].astype(F32))
        block_term(2 * chips[m] + k, put_sum)

    wstep = 256

    def own_work():
        def put(cols, value):
            own[:, cols] = value
        pair_sum(nc - 1, put)
        for i in range(blk // wstep):
            cols = pl.ds(pl.multiple_of(s * blk + i * wstep, 128), wstep)
            acc[:, pl.ds(i * wstep, wstep)] = mm(gt[0], x[:, cols])

    if nc == 4:
        to_x, to_y = (s, 2 * chip_x + k), (s, 2 * chip_y + k)
        top, bottom = pl.ds(0, half), pl.ds(half, half)
        targets = [
            (rt.at[0], to_x), (rt.at[1], to_y),
            (rd.at[0, top], to_x), (rd.at[1, bottom], to_y),
            (rd.at[0, bottom], to_x), (rd.at[1, top], to_y),
        ]

        def send_part(n):
            send(sd.at[n], targets[n][0], rds.at[n], rdr.at[n], targets[n][1])

        def wait_part(n):
            wait_recv(targets[n][0], rds.at[n], rdr.at[n], targets[n][1])

        for m, (a, b) in enumerate(((0, 1), (2, 4), (5, 3))):
            def put(cols, value, a=a, b=b):
                sd[a, :, cols] = value[:half].astype(BF16)
                sd[b, :, cols] = value[half:].astype(BF16)
            pair_sum(m, put)
            for n in (a, b):
                if n < 4:
                    send_part(n)
        own_work()
        for d in first:
            meet(d)
        for n, got in ((4, 1), (5, 0)):
            wait_part(got)
            sd[n] = (sd[n].astype(F32) + rt[got].astype(F32)).astype(BF16)
            send_part(n)
        arrivals = 2
    else:
        for m in range(nc - 1):
            def put(cols, value, m=m):
                sd[m, :, cols] = value.astype(BF16)
            pair_sum(m, put)
            send(sd.at[m], rd.at[m], rds.at[m], rdr.at[m], (s, 2 * chips[m] + k))
        own_work()
        for d in first:
            meet(d)
        arrivals = nc - 1
    for d in rest:
        meet(d)


    def arrived(d):
        wait_recv(gx.at[d], gs.at[d - 1], gr.at[d - 1], (s, j))
        gt[d, :, :head] = gx[d, : 3 * DH]
        packed = gx[d, 3 * DH :].astype(F32)
        gt[d, : 3 * DH // 2, head:] = packed[:, :tail].astype(BF16)
        gt[d, 3 * DH // 2 :, head:] = packed[:, tail:].astype(BF16)
        wait_recv(token_half(d, 1 - k), bx3s.at[d - 1], bx3r.at[d - 1], (s, sibling))

    for d in first:
        arrived(d)
    for i in range(blk // wstep):
        cols = pl.ds(i * wstep, wstep)
        total = acc[:, cols]
        for d in first:
            total = total + mm(gt[d], xg[d - 1, :, cols])
        acc[:, cols] = total
    for d in rest:
        arrived(d)
    square = jnp.zeros((8, wstep), F32)
    for i in range(blk // wstep):
        cols = pl.ds(i * wstep, wstep)
        total = acc[:, cols]
        for d in rest:
            total = total + mm(gt[d], xg[d - 1, :, cols])
        acc[:, cols] = total
        square = square + jnp.sum((total * total).reshape(3 * DH // 8, 8, wstep), axis=0)
    sqt[0] = square[:, :128] + square[:, 128:]
    if flat:
        for i, (a, b) in enumerate(offsets):
            to = (seq_peer(a), t_peer(b))
            send(sqt.at[0], sqt.at[i + 1], ts.at[i], tr.at[i], to)
    else:
        sqz[0] = sqt[0]
        for d in range(1, n_seq):
            send(sqz.at[0], sqz.at[d], zs.at[d - 1], zr.at[d - 1], (seq_peer(d), j))

    def finish():
        if nc == 4:
            for n in range(2, 6):
                wait_part(n)
        else:
            for m in range(arrivals):
                wait_recv(rd.at[m], rds.at[m], rdr.at[m], (s, j))
        total = own[...]
        for m in range(arrivals):
            total = total + rd[m].astype(F32)
        ig_ref[...] = total.astype(BF16)

    if flat:
        finish()
        peers = len(offsets)
    else:
        for d in range(1, n_seq):
            wait_recv(sqz.at[d], zs.at[d - 1], zr.at[d - 1], (s, j))
        total = sqz[0]
        for d in range(1, n_seq):
            total = total + sqz[d]
        sqt[0] = total
        for d in range(1, n_t):
            send(sqt.at[0], sqt.at[d], ts.at[d - 1], tr.at[d - 1], (s, t_peer(d)))
        finish()
        peers = n_t - 1
    for i in range(peers):
        wait_recv(sqt.at[i + 1], ts.at[i], tr.at[i], (s, j))
    total = sqt[0]
    for i in range(peers):
        total = total + sqt[i + 1]
    total = jnp.sum(jnp.sum(total, axis=1, keepdims=True), axis=0, keepdims=True)
    factor = jnp.minimum(1.0, CLIP_RMS * math.sqrt(entries) / jnp.sqrt(total + 1e-06))

    factor_ref[...] = jnp.broadcast_to(factor, (8, 128))
    for copy in sends:
        copy.wait_send()


def write(input_sum, summed, factor_ref, ig_hbm, wg_hbm, scaled, sems):
    copies = [pltpu.make_async_copy(input_sum, ig_hbm, sems.at[0])]
    copies[0].start()
    factor = factor_ref[:1, :1]
    tall = summed.shape[0] // WRITE_CHUNKS
    for i in range(WRITE_CHUNKS):
        part = pl.ds(i * tall, tall)
        scaled[part, :] = (summed[part, :] * factor).astype(BF16)
        copy = pltpu.make_async_copy(scaled.at[part], wg_hbm.at[part], sems.at[i + 1])
        copy.start()
        copies.append(copy)
    for copy in copies:
        copy.wait()


def body(n_seq, n_t, layer_inputs, projection_matrices, result_sensitivity, rate, events):
    rows, width = layer_inputs.shape
    blk, iblk, nc = width // n_seq, width // n_t, n_t // 2
    aligned = iblk % 128 == 0
    w_t = projection_matrices.transpose(1, 2, 0).reshape(3 * DH, width)
    if aligned:
        w_b = result_sensitivity
    else:
        w_b = w_t.reshape(3 * DH, n_t, iblk).transpose(1, 0, 2)
    entries = width * 3 * DH * n_t
    flat = n_seq * n_t <= 64
    peers = n_seq * n_t - 1 if flat else n_t - 1
    dma = pltpu.SemaphoreType.DMA
    vmem = pl.BlockSpec(memory_space=pltpu.VMEM)
    z = n_seq - 1
    input_sum, summed, factor = pl.pallas_call(
        functools.partial(kernel, n_seq, n_t, entries, aligned, flat),
        out_shape=(
            pltpu.VMEM((rows, iblk), BF16),
            pltpu.VMEM((3 * DH, blk), F32),
            pltpu.VMEM((8, 128), F32),
        ),
        in_specs=[pl.BlockSpec(memory_space=pltpu.HBM)] * 6,
        out_specs=(vmem, vmem, vmem),
        scratch_shapes=[
            pltpu.VMEM((rows, width), BF16),
            pltpu.VMEM((3 * DH, width), BF16),
            pltpu.VMEM((8, 128) if aligned else w_b.shape, BF16),
            pltpu.VMEM(result_sensitivity.shape, BF16),
            pltpu.SMEM(rate.shape, F32),
            pltpu.SMEM(events.shape, jnp.int32),
            pltpu.VMEM((z, rows, blk), BF16),
            pltpu.VMEM((rows, 3 * DH), BF16),
            pltpu.VMEM((n_seq, 9 * DH // 2, 128), BF16),
            pltpu.VMEM((n_seq, 3 * DH, rows), BF16),
            pltpu.VMEM((2, n_seq, DH, DH), BF16),
            pltpu.VMEM((nc, rows, iblk), BF16),
            pltpu.VMEM((nc, rows, iblk), BF16),
            pltpu.VMEM((6, rows // 2, iblk) if nc == 4 else (nc - 1, rows, iblk), BF16),
            pltpu.VMEM((2, rows // 2, iblk), BF16),
            pltpu.VMEM((2 if nc == 4 else nc - 1, rows, iblk), BF16),
            pltpu.VMEM((rows, iblk), F32),
            pltpu.VMEM((n_seq, 8, 128), F32),
            pltpu.VMEM((peers + 1, 8, 128), F32),
            dma((2 * LOAD_CHUNKS + 1,)), dma((3,)),
            dma((z,)), dma((z,)),
            dma((z, 3)), dma((z, 3)),
            dma((z,)), dma((z,)),
            dma((z,)), dma((z,)),
            dma((z,)), dma((z,)),
            dma((nc,)), dma((nc,)),
            dma((6 if nc == 4 else nc - 1,)), dma((6 if nc == 4 else nc - 1,)),
            dma((z,)), dma((z,)),
            dma((peers,)), dma((peers,)),
        ],
        compiler_params=pltpu.CompilerParams(
            collective_id=0, has_side_effects=True, vmem_limit_bytes=56 * 1024 * 1024
        ),
    )(layer_inputs, w_t, w_b, result_sensitivity, rate, events)
    whole = pl.BlockSpec(memory_space=pl.ANY)
    input_t, weight_t = pl.pallas_call(
        write,
        out_shape=(
            jax.ShapeDtypeStruct((rows, iblk), BF16),
            jax.ShapeDtypeStruct((3 * DH, blk), BF16),
        ),
        in_specs=[vmem] * 3,
        out_specs=(whole, whole),
        scratch_shapes=[
            pltpu.VMEM((3 * DH, blk), BF16),
            dma((WRITE_CHUNKS + 1,)),
        ],
        compiler_params=pltpu.CompilerParams(vmem_limit_bytes=16 * 1024 * 1024),
    )(input_sum, summed, factor)
    weight_grad = weight_t.reshape(3, DH, blk).transpose(2, 0, 1)
    return input_t.T, weight_grad


def solution(mesh):
    return jax.shard_map(
        functools.partial(body, mesh.shape["seq"], mesh.shape["tensor"]),
        mesh=mesh,
        in_specs=(P("seq", None), P(None, None, "tensor"), P("seq", "tensor"), P("tensor"), P()),
        out_specs=(P("tensor", "seq"), P("seq", None, "tensor")),
        check_vma=False,
    )
```

```python
import functools
import math

import jax
import jax.numpy as jnp
from jax import lax
from jax.experimental import pallas as pl
from jax.experimental.pallas import tpu as pltpu
from jax.sharding import PartitionSpec as P

DH = 96
DROP_LOGARITHM = 0.3
CLIP_RMS = 0.5
MESH = pl.DeviceIdType.MESH
F32 = jnp.float32
BF16 = jnp.bfloat16
LOAD_CHUNKS = 4
WRITE_CHUNKS = 3


def mm(a, b):
    return jnp.dot(a, b, preferred_element_type=F32)


def mm_nt(a, b):
    return lax.dot_general(a, b, (((1,), (1,)), ((), ())), preferred_element_type=F32)


def kernel(
    n_seq, n_t, entries, aligned, flat,
    x_hbm, w_hbm, wb_hbm, o_hbm, rate_hbm, events_hbm,
    ig_ref, acc, factor_ref,
    x, w, wb, o_ref, rate_ref, events_ref,
    xg, g, gx, gt, st, ps, rc, sd, rt, rd, own, sqz, sqt,
    load_sem, small_sem, bx1s, bx1r, bx2s, bx2r, bx3s, bx3r, sts, str_, gs, gr,
    pss, psr, rds, rdr, zs, zr, ts, tr,
):
    rows, width = x_hbm.shape
    blk = width // n_seq
    iblk = width // n_t
    scale = DH ** (-0.5)
    s = lax.axis_index("seq")
    j = lax.axis_index("tensor")
    nc = n_t // 2
    k = lax.rem(j, 2)
    chip = j // 2
    sibling = j + 1 - 2 * k
    group = (j // 8) * 8
    c = lax.rem(j, 8) // 2
    q = blk // 4
    half = rows // 2
    order = sorted(range(1, n_seq), key=lambda d: min(d, n_seq - d))
    first, rest = order[: max(1, n_seq // 2)], order[max(1, n_seq // 2) :]

    def across(n):
        a, b = lax.rem(n, 2), lax.rem(n // 2, 2)
        return n + 1 - 2 * a, n + 2 - 4 * b, n + 3 - 2 * a - 4 * b

    c_x, c_y, c_d = across(c)
    dev_x, dev_y = group + 2 * c_x + k, group + 2 * c_y + k

    wide = width // LOAD_CHUNKS
    loads = []
    for i in range(LOAD_CHUNKS):
        cols = pl.ds(i * wide, wide)
        for n, (src, dst) in enumerate(((x_hbm, x), (w_hbm, w))):
            copy = pltpu.make_async_copy(src.at[:, cols], dst.at[:, cols], load_sem.at[2 * i + n])
            copy.start()
            loads.append(copy)
    smalls = []
    for n, (src, dst) in enumerate(((o_hbm, o_ref), (rate_hbm, rate_ref), (events_hbm, events_ref))):
        copy = pltpu.make_async_copy(src, dst, small_sem.at[n])
        copy.start()
        smalls.append(copy)
    if not aligned:
        wb_copy = pltpu.make_async_copy(wb_hbm, wb, load_sem.at[2 * LOAD_CHUNKS])
        wb_copy.start()

    def seq_peer(d):
        return lax.rem(s + d, n_seq)

    def t_peer(d):
        return lax.rem(j + d, n_t)

    offsets = [(a, b) for a in range(n_seq) for b in range(n_t) if (flat or a * b == 0) and a + b]
    barrier = pltpu.get_barrier_semaphore()
    for a, b in offsets:
        pl.semaphore_signal(barrier, inc=1, device_id=(seq_peer(a), t_peer(b)), device_id_type=MESH)
    pl.semaphore_wait(barrier, len(offsets))

    sends = []

    def send(src, dst, ssem, rsem, device):
        copy = pltpu.make_async_remote_copy(
            src_ref=src, dst_ref=dst, send_sem=ssem, recv_sem=rsem,
            device_id=device, device_id_type=MESH,
        )
        copy.start()
        sends.append(copy)

    def wait_recv(ref, ssem, rsem, device):
        pltpu.make_async_remote_copy(
            src_ref=ref, dst_ref=ref, send_sem=ssem, recv_sem=rsem,
            device_id=device, device_id_type=MESH,
        ).wait_recv()

    def piece(d, core, chip_col):
        return xg.at[
            d - 1,
            pl.ds(pl.multiple_of(core * half, 32), half),
            pl.ds(pl.multiple_of(chip_col * q, 128), q),
        ]

    def quarter(d, chip_col, low):
        start = pl.multiple_of(k * half + low * (half // 2), 16)
        return xg.at[d - 1, pl.ds(start, half // 2), pl.ds(pl.multiple_of(chip_col * q, 128), q)]

    def share(d):
        wait_recv(piece(d, k, c), bx1s.at[d - 1], bx1r.at[d - 1], (s, j))
        mine = piece(d, k, c)
        send(mine, mine, bx2s.at[d - 1, 0], bx2r.at[d - 1, 0], (s, dev_x))
        send(mine, mine, bx2s.at[d - 1, 1], bx2r.at[d - 1, 1], (s, dev_y))

    def forward(d):
        wait_recv(piece(d, k, c_x), bx2s.at[d - 1, 0], bx2r.at[d - 1, 0], (s, dev_x))
        top = quarter(d, c_x, 0)
        send(top, top, bx2s.at[d - 1, 2], bx2r.at[d - 1, 2], (s, dev_y))
        wait_recv(piece(d, k, c_y), bx2s.at[d - 1, 1], bx2r.at[d - 1, 1], (s, dev_y))
        bottom = quarter(d, c_y, 1)
        send(bottom, bottom, bx2s.at[d - 1, 3], bx2r.at[d - 1, 3], (s, dev_x))

    def meet(d):
        wait_recv(quarter(d, c_d, 0), bx2s.at[d - 1, 2], bx2r.at[d - 1, 2], (s, dev_y))
        wait_recv(quarter(d, c_d, 1), bx2s.at[d - 1, 3], bx2r.at[d - 1, 3], (s, dev_x))
        send(token_half(d, k), token_half(d, k), bx3s.at[d - 1], bx3r.at[d - 1], (s, sibling))

    def token_half(d, core):
        return xg.at[d - 1, pl.ds(pl.multiple_of(core * half, 32), half), :]

    def exchange(d):
        src = x_hbm.at[
            pl.ds(pl.multiple_of(k * half, 32), half),
            pl.ds(pl.multiple_of(seq_peer(d) * blk + c * q, 128), q),
        ]
        send(src, piece(d, k, c), bx1s.at[d - 1], bx1r.at[d - 1], (seq_peer(d), j))

    for d in order:
        exchange(d)

    proj = jnp.zeros((3 * DH, rows), F32)
    for i in range(LOAD_CHUNKS):
        cols = pl.ds(i * wide, wide)
        loads[2 * i].wait()
        loads[2 * i + 1].wait()
        proj = proj + mm_nt(w[:, cols], x[:, cols])
    q_t = (proj[:DH] * scale).astype(BF16)
    k_t = proj[DH : 2 * DH].astype(BF16)
    v_t = proj[2 * DH :].astype(BF16)
    for copy in smalls:
        copy.wait()
    o = o_ref[...]
    o_t = o.astype(F32).T.astype(BF16)
    q_r = q_t.astype(F32).T.astype(BF16)
    v_r = v_t.astype(F32).T.astype(BF16)

    rate = rate_ref[0]
    n_events = events_ref.shape[0]
    base = s * rows
    lane = lax.broadcasted_iota(jnp.int32, (1, rows), 1)

    def events_in(low, high):
        total = jnp.zeros(jnp.broadcast_shapes(jnp.shape(low), jnp.shape(high)), F32)
        for n in range(n_events):
            e = events_ref[n]
            total = total + jnp.where((e > low) & (e <= high), 1.0, 0.0)
        return total

    last = jnp.full((1, rows), rows - 1, jnp.int32) + base
    before = jnp.full((1, rows), -1, jnp.int32) + base
    here = lane + base
    head_w = jnp.exp(-(rate * (lane + 1).astype(F32) + DROP_LOGARITHM * events_in(before, here)))
    tail_w = jnp.exp(
        -(rate * (rows - 1 - lane).astype(F32) + DROP_LOGARITHM * events_in(here, last))
    )

    st[0, 0] = mm((k_t.astype(F32) * tail_w).astype(BF16), v_r).astype(BF16)
    st[1, 0] = mm((q_t.astype(F32) * head_w).astype(BF16), o).astype(BF16)
    for d in range(1, n_seq):
        earlier = jnp.where(seq_peer(d) < s, 1, 0)
        send(st.at[earlier, 0], st.at[0, d], sts.at[d - 1], str_.at[d - 1], (seq_peer(d), j))

    for d in first:
        share(d)

    t_idx = lax.broadcasted_iota(jnp.int32, (rows, rows), 0)
    s_idx = lax.broadcasted_iota(jnp.int32, (rows, rows), 1)
    decay = rate * (t_idx - s_idx).astype(F32) + DROP_LOGARITHM * events_in(
        s_idx + base, t_idx + base
    )
    weight = jnp.where(t_idx >= s_idx, jnp.exp(-jnp.maximum(decay, 0.0)), 0.0)
    scores = (mm(q_r, k_t) * weight).astype(BF16)
    dscores = (mm(o, v_t) * weight).astype(BF16)
    dq_t = mm_nt(k_t, dscores)
    dk_t = mm(q_t, dscores)
    dv_t = mm(o_t, scores)

    for d in rest:
        share(d)

    prefix = jnp.zeros((DH, DH), F32)
    suffix = jnp.zeros((DH, DH), F32)
    zero = jnp.zeros((1, DH), jnp.int32)
    for d in range(1, n_seq):
        wait_recv(st.at[0, d], sts.at[d - 1], str_.at[d - 1], (s, j))
        src = lax.rem(s + n_seq - d, n_seq)
        state = st[0, d].astype(F32)
        low = jnp.minimum(src, s)
        high = jnp.maximum(src, s)
        gap = rate * ((high - low - 1) * rows).astype(F32) + DROP_LOGARITHM * events_in(
            zero + ((low + 1) * rows - 1), zero + (high * rows - 1)
        )
        state = state * jnp.exp(-gap)
        is_fwd = (zero + src) < (zero + s)
        prefix = prefix + jnp.where(is_fwd, state, 0.0)
        suffix = suffix + jnp.where(is_fwd, 0.0, state)
    dq_t = dq_t + mm(prefix.astype(BF16), o_t) * head_w
    dk_t = dk_t + mm(suffix.astype(BF16), v_t) * tail_w
    dv_t = dv_t + mm(suffix.T.astype(BF16), k_t) * tail_w
    grads_t = jnp.concatenate([dq_t * scale, dk_t, dv_t], axis=0)
    gt[0] = grads_t.astype(BF16)
    g[...] = grads_t.T.astype(BF16)
    head, tail = 128, rows - 128
    low, high = grads_t[: 3 * DH // 2, head:], grads_t[3 * DH // 2 :, head:]
    gx[0, : 3 * DH] = grads_t[:, :head].astype(BF16)
    gx[0, 3 * DH :] = jnp.concatenate([low, high], axis=1).astype(BF16)
    for d in range(1, n_seq):
        send(gx.at[0], gx.at[d], gs.at[d - 1], gr.at[d - 1], (seq_peer(d), j))

    if not aligned:
        wb_copy.wait()

    def block_term(owner, put):
        if aligned:
            put(pl.ds(0, iblk), mm(g[...], w[:, pl.ds(pl.multiple_of(owner * iblk, 128), iblk)]))
        else:
            put(pl.ds(0, iblk), mm(g[...], wb[owner]))

    if nc == 4:
        chip_x, chip_y, chip_d = across(chip)
        chips = [chip_d, chip_x, chip_y, chip]
    else:
        chips = [lax.rem(chip + m, nc) for m in range(1, nc + 1)]
    for m in range(nc):
        def put(cols, value, m=m):
            ps[m, :, cols] = value.astype(BF16)
        block_term(2 * chips[m] + 1 - k, put)
        send(ps.at[m], rc.at[m], pss.at[m], psr.at[m], (s, sibling))
    for d in first:
        forward(d)

    def pair_sum(m, put):
        wait_recv(rc.at[m], pss.at[m], psr.at[m], (s, sibling))
        def put_sum(cols, value):
            put(cols, value + rc[m, :, cols].astype(F32))
        block_term(2 * chips[m] + k, put_sum)

    wstep = 256

    def own_work():
        def put(cols, value):
            own[:, cols] = value
        pair_sum(nc - 1, put)
        for i in range(blk // wstep):
            cols = pl.ds(pl.multiple_of(s * blk + i * wstep, 128), wstep)
            acc[:, pl.ds(i * wstep, wstep)] = mm(gt[0], x[:, cols])

    if nc == 4:
        to_x, to_y = (s, 2 * chip_x + k), (s, 2 * chip_y + k)
        top, bottom = pl.ds(0, half), pl.ds(half, half)
        targets = [
            (rt.at[0], to_x), (rt.at[1], to_y),
            (rd.at[0, top], to_x), (rd.at[1, bottom], to_y),
            (rd.at[0, bottom], to_x), (rd.at[1, top], to_y),
        ]

        def send_part(n):
            send(sd.at[n], targets[n][0], rds.at[n], rdr.at[n], targets[n][1])

        def wait_part(n):
            wait_recv(targets[n][0], rds.at[n], rdr.at[n], targets[n][1])

        for m, (a, b) in enumerate(((0, 1), (2, 4), (5, 3))):
            def put(cols, value, a=a, b=b):
                sd[a, :, cols] = value[:half].astype(BF16)
                sd[b, :, cols] = value[half:].astype(BF16)
            pair_sum(m, put)
            for n in (a, b):
                if n < 4:
                    send_part(n)
        for d in rest:
            forward(d)
        own_work()
        for d in first:
            meet(d)
        for n, got in ((4, 1), (5, 0)):
            wait_part(got)
            sd[n] = (sd[n].astype(F32) + rt[got].astype(F32)).astype(BF16)
            send_part(n)
        arrivals = 2
    else:
        for m in range(nc - 1):
            def put(cols, value, m=m):
                sd[m, :, cols] = value.astype(BF16)
            pair_sum(m, put)
            send(sd.at[m], rd.at[m], rds.at[m], rdr.at[m], (s, 2 * chips[m] + k))
        for d in rest:
            forward(d)
        own_work()
        for d in first:
            meet(d)
        arrivals = nc - 1
    for d in rest:
        meet(d)


    def arrived(d):
        wait_recv(gx.at[d], gs.at[d - 1], gr.at[d - 1], (s, j))
        gt[d, :, :head] = gx[d, : 3 * DH]
        packed = gx[d, 3 * DH :].astype(F32)
        gt[d, : 3 * DH // 2, head:] = packed[:, :tail].astype(BF16)
        gt[d, 3 * DH // 2 :, head:] = packed[:, tail:].astype(BF16)
        wait_recv(token_half(d, 1 - k), bx3s.at[d - 1], bx3r.at[d - 1], (s, sibling))

    for d in first:
        arrived(d)
    for i in range(blk // wstep):
        cols = pl.ds(i * wstep, wstep)
        total = acc[:, cols]
        for d in first:
            total = total + mm(gt[d], xg[d - 1, :, cols])
        acc[:, cols] = total
    for d in rest:
        arrived(d)
    square = jnp.zeros((8, wstep), F32)
    for i in range(blk // wstep):
        cols = pl.ds(i * wstep, wstep)
        total = acc[:, cols]
        for d in rest:
            total = total + mm(gt[d], xg[d - 1, :, cols])
        acc[:, cols] = total
        square = square + jnp.sum((total * total).reshape(3 * DH // 8, 8, wstep), axis=0)
    sqt[0] = square[:, :128] + square[:, 128:]
    if flat:
        for i, (a, b) in enumerate(offsets):
            to = (seq_peer(a), t_peer(b))
            send(sqt.at[0], sqt.at[i + 1], ts.at[i], tr.at[i], to)
    else:
        sqz[0] = sqt[0]
        for d in range(1, n_seq):
            send(sqz.at[0], sqz.at[d], zs.at[d - 1], zr.at[d - 1], (seq_peer(d), j))

    def finish():
        if nc == 4:
            for n in range(2, 6):
                wait_part(n)
        else:
            for m in range(arrivals):
                wait_recv(rd.at[m], rds.at[m], rdr.at[m], (s, j))
        total = own[...]
        for m in range(arrivals):
            total = total + rd[m].astype(F32)
        ig_ref[...] = total.astype(BF16)

    if flat:
        finish()
        peers = len(offsets)
    else:
        for d in range(1, n_seq):
            wait_recv(sqz.at[d], zs.at[d - 1], zr.at[d - 1], (s, j))
        total = sqz[0]
        for d in range(1, n_seq):
            total = total + sqz[d]
        sqt[0] = total
        for d in range(1, n_t):
            send(sqt.at[0], sqt.at[d], ts.at[d - 1], tr.at[d - 1], (s, t_peer(d)))
        finish()
        peers = n_t - 1
    for i in range(peers):
        wait_recv(sqt.at[i + 1], ts.at[i], tr.at[i], (s, j))
    total = sqt[0]
    for i in range(peers):
        total = total + sqt[i + 1]
    total = jnp.sum(jnp.sum(total, axis=1, keepdims=True), axis=0, keepdims=True)
    factor = jnp.minimum(1.0, CLIP_RMS * math.sqrt(entries) / jnp.sqrt(total + 1e-06))

    factor_ref[...] = jnp.broadcast_to(factor, (8, 128))
    for copy in sends:
        copy.wait_send()


def write(input_sum, summed, factor_ref, ig_hbm, wg_hbm, scaled, sems):
    copies = [pltpu.make_async_copy(input_sum, ig_hbm, sems.at[0])]
    copies[0].start()
    factor = factor_ref[:1, :1]
    tall = summed.shape[0] // WRITE_CHUNKS
    for i in range(WRITE_CHUNKS):
        part = pl.ds(i * tall, tall)
        scaled[part, :] = (summed[part, :] * factor).astype(BF16)
        copy = pltpu.make_async_copy(scaled.at[part], wg_hbm.at[part], sems.at[i + 1])
        copy.start()
        copies.append(copy)
    for copy in copies:
        copy.wait()


def body(n_seq, n_t, layer_inputs, projection_matrices, result_sensitivity, rate, events):
    rows, width = layer_inputs.shape
    blk, iblk, nc = width // n_seq, width // n_t, n_t // 2
    aligned = iblk % 128 == 0
    w_t = projection_matrices.transpose(1, 2, 0).reshape(3 * DH, width)
    if aligned:
        w_b = result_sensitivity
    else:
        w_b = w_t.reshape(3 * DH, n_t, iblk).transpose(1, 0, 2)
    entries = width * 3 * DH * n_t
    flat = n_seq * n_t <= 64
    peers = n_seq * n_t - 1 if flat else n_t - 1
    dma = pltpu.SemaphoreType.DMA
    vmem = pl.BlockSpec(memory_space=pltpu.VMEM)
    z = n_seq - 1
    input_sum, summed, factor = pl.pallas_call(
        functools.partial(kernel, n_seq, n_t, entries, aligned, flat),
        out_shape=(
            pltpu.VMEM((rows, iblk), BF16),
            pltpu.VMEM((3 * DH, blk), F32),
            pltpu.VMEM((8, 128), F32),
        ),
        in_specs=[pl.BlockSpec(memory_space=pltpu.HBM)] * 6,
        out_specs=(vmem, vmem, vmem),
        scratch_shapes=[
            pltpu.VMEM((rows, width), BF16),
            pltpu.VMEM((3 * DH, width), BF16),
            pltpu.VMEM((8, 128) if aligned else w_b.shape, BF16),
            pltpu.VMEM(result_sensitivity.shape, BF16),
            pltpu.SMEM(rate.shape, F32),
            pltpu.SMEM(events.shape, jnp.int32),
            pltpu.VMEM((z, rows, blk), BF16),
            pltpu.VMEM((rows, 3 * DH), BF16),
            pltpu.VMEM((n_seq, 9 * DH // 2, 128), BF16),
            pltpu.VMEM((n_seq, 3 * DH, rows), BF16),
            pltpu.VMEM((2, n_seq, DH, DH), BF16),
            pltpu.VMEM((nc, rows, iblk), BF16),
            pltpu.VMEM((nc, rows, iblk), BF16),
            pltpu.VMEM((6, rows // 2, iblk) if nc == 4 else (nc - 1, rows, iblk), BF16),
            pltpu.VMEM((2, rows // 2, iblk), BF16),
            pltpu.VMEM((2 if nc == 4 else nc - 1, rows, iblk), BF16),
            pltpu.VMEM((rows, iblk), F32),
            pltpu.VMEM((n_seq, 8, 128), F32),
            pltpu.VMEM((peers + 1, 8, 128), F32),
            dma((2 * LOAD_CHUNKS + 1,)), dma((3,)),
            dma((z,)), dma((z,)),
            dma((z, 4)), dma((z, 4)),
            dma((z,)), dma((z,)),
            dma((z,)), dma((z,)),
            dma((z,)), dma((z,)),
            dma((nc,)), dma((nc,)),
            dma((6 if nc == 4 else nc - 1,)), dma((6 if nc == 4 else nc - 1,)),
            dma((z,)), dma((z,)),
            dma((peers,)), dma((peers,)),
        ],
        compiler_params=pltpu.CompilerParams(
            collective_id=0, has_side_effects=True, vmem_limit_bytes=56 * 1024 * 1024
        ),
    )(layer_inputs, w_t, w_b, result_sensitivity, rate, events)
    whole = pl.BlockSpec(memory_space=pl.ANY)
    input_t, weight_t = pl.pallas_call(
        write,
        out_shape=(
            jax.ShapeDtypeStruct((rows, iblk), BF16),
            jax.ShapeDtypeStruct((3 * DH, blk), BF16),
        ),
        in_specs=[vmem] * 3,
        out_specs=(whole, whole),
        scratch_shapes=[
            pltpu.VMEM((3 * DH, blk), BF16),
            dma((WRITE_CHUNKS + 1,)),
        ],
        compiler_params=pltpu.CompilerParams(vmem_limit_bytes=16 * 1024 * 1024),
    )(input_sum, summed, factor)
    weight_grad = weight_t.reshape(3, DH, blk).transpose(2, 0, 1)
    return input_t.T, weight_grad


def solution(mesh):
    return jax.shard_map(
        functools.partial(body, mesh.shape["seq"], mesh.shape["tensor"]),
        mesh=mesh,
        in_specs=(P("seq", None), P(None, None, "tensor"), P("seq", "tensor"), P("tensor"), P()),
        out_specs=(P("tensor", "seq"), P("seq", None, "tensor")),
        check_vma=False,
    )
```

```python
import functools
import math

import jax
import jax.numpy as jnp
from jax import lax
from jax.experimental import pallas as pl
from jax.experimental.pallas import tpu as pltpu
from jax.sharding import PartitionSpec as P

DH = 96
DROP_LOGARITHM = 0.3
CLIP_RMS = 0.5
MESH = pl.DeviceIdType.MESH
F32 = jnp.float32
BF16 = jnp.bfloat16
LOAD_CHUNKS = 4
WRITE_CHUNKS = 3


def mm(a, b):
    return jnp.dot(a, b, preferred_element_type=F32)


def mm_nt(a, b):
    return lax.dot_general(a, b, (((1,), (1,)), ((), ())), preferred_element_type=F32)


def kernel(
    n_seq, n_t, entries, aligned, flat,
    x_hbm, w_hbm, wb_hbm, o_hbm, rate_hbm, events_hbm,
    ig_ref, acc, factor_ref,
    x, w, wb, o_ref, rate_ref, events_ref,
    xg, g, gx, gt, st, ps, rc, sd, rd, own, sqz, sqt,
    load_sem, small_sem, bx1s, bx1r, bx2s, bx2r, bx3s, bx3r, sts, str_, gs, gr,
    pss, psr, rds, rdr, zs, zr, ts, tr,
):
    rows, width = x_hbm.shape
    blk = width // n_seq
    iblk = width // n_t
    scale = DH ** (-0.5)
    s = lax.axis_index("seq")
    j = lax.axis_index("tensor")
    nc = n_t // 2
    k = lax.rem(j, 2)
    chip = j // 2
    sibling = j + 1 - 2 * k
    group = (j // 8) * 8
    c = lax.rem(j, 8) // 2
    q = blk // 4
    half = rows // 2
    order = sorted(range(1, n_seq), key=lambda d: min(d, n_seq - d))
    first, rest = order[: max(1, n_seq // 2)], order[max(1, n_seq // 2) :]

    def across(n):
        a, b = lax.rem(n, 2), lax.rem(n // 2, 2)
        return n + 1 - 2 * a, n + 2 - 4 * b, n + 3 - 2 * a - 4 * b

    c_x, c_y, c_d = across(c)
    dev_x, dev_y, dev_d = group + 2 * c_x + k, group + 2 * c_y + k, group + 2 * c_d + k

    wide = width // LOAD_CHUNKS
    loads = []
    for i in range(LOAD_CHUNKS):
        cols = pl.ds(i * wide, wide)
        for n, (src, dst) in enumerate(((x_hbm, x), (w_hbm, w))):
            copy = pltpu.make_async_copy(src.at[:, cols], dst.at[:, cols], load_sem.at[2 * i + n])
            copy.start()
            loads.append(copy)
    smalls = []
    for n, (src, dst) in enumerate(((o_hbm, o_ref), (rate_hbm, rate_ref), (events_hbm, events_ref))):
        copy = pltpu.make_async_copy(src, dst, small_sem.at[n])
        copy.start()
        smalls.append(copy)
    if not aligned:
        wb_copy = pltpu.make_async_copy(wb_hbm, wb, load_sem.at[2 * LOAD_CHUNKS])
        wb_copy.start()

    def seq_peer(d):
        return lax.rem(s + d, n_seq)

    def t_peer(d):
        return lax.rem(j + d, n_t)

    offsets = [(a, b) for a in range(n_seq) for b in range(n_t) if (flat or a * b == 0) and a + b]
    barrier = pltpu.get_barrier_semaphore()
    for a, b in offsets:
        pl.semaphore_signal(barrier, inc=1, device_id=(seq_peer(a), t_peer(b)), device_id_type=MESH)
    pl.semaphore_wait(barrier, len(offsets))

    sends = []

    def send(src, dst, ssem, rsem, device):
        copy = pltpu.make_async_remote_copy(
            src_ref=src, dst_ref=dst, send_sem=ssem, recv_sem=rsem,
            device_id=device, device_id_type=MESH,
        )
        copy.start()
        sends.append(copy)

    def wait_recv(ref, ssem, rsem, device):
        pltpu.make_async_remote_copy(
            src_ref=ref, dst_ref=ref, send_sem=ssem, recv_sem=rsem,
            device_id=device, device_id_type=MESH,
        ).wait_recv()

    def piece(d, core, chip_col):
        return xg.at[
            d - 1,
            pl.ds(pl.multiple_of(core * half, 32), half),
            pl.ds(pl.multiple_of(chip_col * q, 128), q),
        ]

    def share(d):
        wait_recv(piece(d, k, c), bx1s.at[d - 1], bx1r.at[d - 1], (s, j))
        mine = piece(d, k, c)
        send(mine, mine, bx2s.at[d - 1, 2], bx2r.at[d - 1, 2], (s, dev_d))
        send(mine, mine, bx2s.at[d - 1, 0], bx2r.at[d - 1, 0], (s, dev_x))
        send(mine, mine, bx2s.at[d - 1, 1], bx2r.at[d - 1, 1], (s, dev_y))

    def meet(d):
        for n, (col, dev) in enumerate(((c_x, dev_x), (c_y, dev_y), (c_d, dev_d))):
            wait_recv(piece(d, k, col), bx2s.at[d - 1, n], bx2r.at[d - 1, n], (s, dev))
        send(token_half(d, k), token_half(d, k), bx3s.at[d - 1], bx3r.at[d - 1], (s, sibling))

    def token_half(d, core):
        return xg.at[d - 1, pl.ds(pl.multiple_of(core * half, 32), half), :]

    def exchange(d):
        src = x_hbm.at[
            pl.ds(pl.multiple_of(k * half, 32), half),
            pl.ds(pl.multiple_of(seq_peer(d) * blk + c * q, 128), q),
        ]
        send(src, piece(d, k, c), bx1s.at[d - 1], bx1r.at[d - 1], (seq_peer(d), j))

    for d in order:
        exchange(d)

    proj = jnp.zeros((3 * DH, rows), F32)
    for i in range(LOAD_CHUNKS):
        cols = pl.ds(i * wide, wide)
        loads[2 * i].wait()
        loads[2 * i + 1].wait()
        proj = proj + mm_nt(w[:, cols], x[:, cols])
    q_t = (proj[:DH] * scale).astype(BF16)
    k_t = proj[DH : 2 * DH].astype(BF16)
    v_t = proj[2 * DH :].astype(BF16)
    for copy in smalls:
        copy.wait()
    o = o_ref[...]
    o_t = o.astype(F32).T.astype(BF16)
    q_r = q_t.astype(F32).T.astype(BF16)
    v_r = v_t.astype(F32).T.astype(BF16)

    rate = rate_ref[0]
    n_events = events_ref.shape[0]
    base = s * rows
    lane = lax.broadcasted_iota(jnp.int32, (1, rows), 1)

    def events_in(low, high):
        total = jnp.zeros(jnp.broadcast_shapes(jnp.shape(low), jnp.shape(high)), F32)
        for n in range(n_events):
            e = events_ref[n]
            total = total + jnp.where((e > low) & (e <= high), 1.0, 0.0)
        return total

    last = jnp.full((1, rows), rows - 1, jnp.int32) + base
    before = jnp.full((1, rows), -1, jnp.int32) + base
    here = lane + base
    head_w = jnp.exp(-(rate * (lane + 1).astype(F32) + DROP_LOGARITHM * events_in(before, here)))
    tail_w = jnp.exp(
        -(rate * (rows - 1 - lane).astype(F32) + DROP_LOGARITHM * events_in(here, last))
    )

    st[0, 0] = mm((k_t.astype(F32) * tail_w).astype(BF16), v_r).astype(BF16)
    st[1, 0] = mm((q_t.astype(F32) * head_w).astype(BF16), o).astype(BF16)
    for d in range(1, n_seq):
        earlier = jnp.where(seq_peer(d) < s, 1, 0)
        send(st.at[earlier, 0], st.at[0, d], sts.at[d - 1], str_.at[d - 1], (seq_peer(d), j))

    for d in first:
        share(d)

    t_idx = lax.broadcasted_iota(jnp.int32, (rows, rows), 0)
    s_idx = lax.broadcasted_iota(jnp.int32, (rows, rows), 1)
    decay = rate * (t_idx - s_idx).astype(F32) + DROP_LOGARITHM * events_in(
        s_idx + base, t_idx + base
    )
    weight = jnp.where(t_idx >= s_idx, jnp.exp(-jnp.maximum(decay, 0.0)), 0.0)
    scores = (mm(q_r, k_t) * weight).astype(BF16)
    dscores = (mm(o, v_t) * weight).astype(BF16)
    dq_t = mm_nt(k_t, dscores)
    dk_t = mm(q_t, dscores)
    dv_t = mm(o_t, scores)

    for d in rest:
        share(d)

    prefix = jnp.zeros((DH, DH), F32)
    suffix = jnp.zeros((DH, DH), F32)
    zero = jnp.zeros((1, DH), jnp.int32)
    for d in range(1, n_seq):
        wait_recv(st.at[0, d], sts.at[d - 1], str_.at[d - 1], (s, j))
        src = lax.rem(s + n_seq - d, n_seq)
        state = st[0, d].astype(F32)
        low = jnp.minimum(src, s)
        high = jnp.maximum(src, s)
        gap = rate * ((high - low - 1) * rows).astype(F32) + DROP_LOGARITHM * events_in(
            zero + ((low + 1) * rows - 1), zero + (high * rows - 1)
        )
        state = state * jnp.exp(-gap)
        is_fwd = (zero + src) < (zero + s)
        prefix = prefix + jnp.where(is_fwd, state, 0.0)
        suffix = suffix + jnp.where(is_fwd, 0.0, state)
    dq_t = dq_t + mm(prefix.astype(BF16), o_t) * head_w
    dk_t = dk_t + mm(suffix.astype(BF16), v_t) * tail_w
    dv_t = dv_t + mm(suffix.T.astype(BF16), k_t) * tail_w
    grads_t = jnp.concatenate([dq_t * scale, dk_t, dv_t], axis=0)
    gt[0] = grads_t.astype(BF16)
    g[...] = grads_t.T.astype(BF16)
    head, tail = 128, rows - 128
    low, high = grads_t[: 3 * DH // 2, head:], grads_t[3 * DH // 2 :, head:]
    gx[0, : 3 * DH] = grads_t[:, :head].astype(BF16)
    gx[0, 3 * DH :] = jnp.concatenate([low, high], axis=1).astype(BF16)
    for d in range(1, n_seq):
        send(gx.at[0], gx.at[d], gs.at[d - 1], gr.at[d - 1], (seq_peer(d), j))

    if not aligned:
        wb_copy.wait()

    def block_term(owner, put):
        if aligned:
            put(pl.ds(0, iblk), mm(g[...], w[:, pl.ds(pl.multiple_of(owner * iblk, 128), iblk)]))
        else:
            put(pl.ds(0, iblk), mm(g[...], wb[owner]))

    if nc == 4:
        chip_x, chip_y, chip_d = across(chip)
        chips = [chip_d, chip_x, chip_y, chip]
    else:
        chips = [lax.rem(chip + m, nc) for m in range(1, nc + 1)]
    for m in range(nc):
        def put(cols, value, m=m):
            ps[m, :, cols] = value.astype(BF16)
        block_term(2 * chips[m] + 1 - k, put)
        send(ps.at[m], rc.at[m], pss.at[m], psr.at[m], (s, sibling))

    def pair_sum(m, put):
        wait_recv(rc.at[m], pss.at[m], psr.at[m], (s, sibling))
        def put_sum(cols, value):
            put(cols, value + rc[m, :, cols].astype(F32))
        block_term(2 * chips[m] + k, put_sum)

    wstep = 256

    def own_work():
        def put(cols, value):
            own[:, cols] = value
        pair_sum(nc - 1, put)
        for i in range(blk // wstep):
            cols = pl.ds(pl.multiple_of(s * blk + i * wstep, 128), wstep)
            acc[:, pl.ds(i * wstep, wstep)] = mm(gt[0], x[:, cols])

    for m in range(nc - 1):
        def put(cols, value, m=m):
            sd[m, :, cols] = value.astype(BF16)
        pair_sum(m, put)
        send(sd.at[m], rd.at[m], rds.at[m], rdr.at[m], (s, 2 * chips[m] + k))
    own_work()
    for d in first:
        meet(d)
    for d in rest:
        meet(d)


    def arrived(d):
        wait_recv(gx.at[d], gs.at[d - 1], gr.at[d - 1], (s, j))
        gt[d, :, :head] = gx[d, : 3 * DH]
        packed = gx[d, 3 * DH :].astype(F32)
        gt[d, : 3 * DH // 2, head:] = packed[:, :tail].astype(BF16)
        gt[d, 3 * DH // 2 :, head:] = packed[:, tail:].astype(BF16)
        wait_recv(token_half(d, 1 - k), bx3s.at[d - 1], bx3r.at[d - 1], (s, sibling))

    for d in first:
        arrived(d)
    for i in range(blk // wstep):
        cols = pl.ds(i * wstep, wstep)
        total = acc[:, cols]
        for d in first:
            total = total + mm(gt[d], xg[d - 1, :, cols])
        acc[:, cols] = total
    for d in rest:
        arrived(d)
    square = jnp.zeros((8, wstep), F32)
    for i in range(blk // wstep):
        cols = pl.ds(i * wstep, wstep)
        total = acc[:, cols]
        for d in rest:
            total = total + mm(gt[d], xg[d - 1, :, cols])
        acc[:, cols] = total
        square = square + jnp.sum((total * total).reshape(3 * DH // 8, 8, wstep), axis=0)
    sqt[0] = square[:, :128] + square[:, 128:]
    if flat:
        for i, (a, b) in enumerate(offsets):
            to = (seq_peer(a), t_peer(b))
            send(sqt.at[0], sqt.at[i + 1], ts.at[i], tr.at[i], to)
    else:
        sqz[0] = sqt[0]
        for d in range(1, n_seq):
            send(sqz.at[0], sqz.at[d], zs.at[d - 1], zr.at[d - 1], (seq_peer(d), j))

    def finish():
        for m in range(nc - 1):
            wait_recv(rd.at[m], rds.at[m], rdr.at[m], (s, j))
        total = own[...]
        for m in range(nc - 1):
            total = total + rd[m].astype(F32)
        ig_ref[...] = total.astype(BF16)

    if flat:
        finish()
        peers = len(offsets)
    else:
        for d in range(1, n_seq):
            wait_recv(sqz.at[d], zs.at[d - 1], zr.at[d - 1], (s, j))
        total = sqz[0]
        for d in range(1, n_seq):
            total = total + sqz[d]
        sqt[0] = total
        for d in range(1, n_t):
            send(sqt.at[0], sqt.at[d], ts.at[d - 1], tr.at[d - 1], (s, t_peer(d)))
        finish()
        peers = n_t - 1
    for i in range(peers):
        wait_recv(sqt.at[i + 1], ts.at[i], tr.at[i], (s, j))
    total = sqt[0]
    for i in range(peers):
        total = total + sqt[i + 1]
    total = jnp.sum(jnp.sum(total, axis=1, keepdims=True), axis=0, keepdims=True)
    factor = jnp.minimum(1.0, CLIP_RMS * math.sqrt(entries) / jnp.sqrt(total + 1e-06))

    factor_ref[...] = jnp.broadcast_to(factor, (8, 128))
    for copy in sends:
        copy.wait_send()


def write(input_sum, summed, factor_ref, ig_hbm, wg_hbm, scaled, sems):
    copies = [pltpu.make_async_copy(input_sum, ig_hbm, sems.at[0])]
    copies[0].start()
    factor = factor_ref[:1, :1]
    tall = summed.shape[0] // WRITE_CHUNKS
    for i in range(WRITE_CHUNKS):
        part = pl.ds(i * tall, tall)
        scaled[part, :] = (summed[part, :] * factor).astype(BF16)
        copy = pltpu.make_async_copy(scaled.at[part], wg_hbm.at[part], sems.at[i + 1])
        copy.start()
        copies.append(copy)
    for copy in copies:
        copy.wait()


def body(n_seq, n_t, layer_inputs, projection_matrices, result_sensitivity, rate, events):
    rows, width = layer_inputs.shape
    blk, iblk, nc = width // n_seq, width // n_t, n_t // 2
    aligned = iblk % 128 == 0
    w_t = projection_matrices.transpose(1, 2, 0).reshape(3 * DH, width)
    if aligned:
        w_b = result_sensitivity
    else:
        w_b = w_t.reshape(3 * DH, n_t, iblk).transpose(1, 0, 2)
    entries = width * 3 * DH * n_t
    flat = n_seq * n_t <= 64
    peers = n_seq * n_t - 1 if flat else n_t - 1
    dma = pltpu.SemaphoreType.DMA
    vmem = pl.BlockSpec(memory_space=pltpu.VMEM)
    z = n_seq - 1
    input_sum, summed, factor = pl.pallas_call(
        functools.partial(kernel, n_seq, n_t, entries, aligned, flat),
        out_shape=(
            pltpu.VMEM((rows, iblk), BF16),
            pltpu.VMEM((3 * DH, blk), F32),
            pltpu.VMEM((8, 128), F32),
        ),
        in_specs=[pl.BlockSpec(memory_space=pltpu.HBM)] * 6,
        out_specs=(vmem, vmem, vmem),
        scratch_shapes=[
            pltpu.VMEM((rows, width), BF16),
            pltpu.VMEM((3 * DH, width), BF16),
            pltpu.VMEM((8, 128) if aligned else w_b.shape, BF16),
            pltpu.VMEM(result_sensitivity.shape, BF16),
            pltpu.SMEM(rate.shape, F32),
            pltpu.SMEM(events.shape, jnp.int32),
            pltpu.VMEM((z, rows, blk), BF16),
            pltpu.VMEM((rows, 3 * DH), BF16),
            pltpu.VMEM((n_seq, 9 * DH // 2, 128), BF16),
            pltpu.VMEM((n_seq, 3 * DH, rows), BF16),
            pltpu.VMEM((2, n_seq, DH, DH), BF16),
            pltpu.VMEM((nc, rows, iblk), BF16),
            pltpu.VMEM((nc, rows, iblk), BF16),
            pltpu.VMEM((nc - 1, rows, iblk), BF16),
            pltpu.VMEM((nc - 1, rows, iblk), BF16),
            pltpu.VMEM((rows, iblk), F32),
            pltpu.VMEM((n_seq, 8, 128), F32),
            pltpu.VMEM((peers + 1, 8, 128), F32),
            dma((2 * LOAD_CHUNKS + 1,)), dma((3,)),
            dma((z,)), dma((z,)),
            dma((z, 3)), dma((z, 3)),
            dma((z,)), dma((z,)),
            dma((z,)), dma((z,)),
            dma((z,)), dma((z,)),
            dma((nc,)), dma((nc,)),
            dma((nc - 1,)), dma((nc - 1,)),
            dma((z,)), dma((z,)),
            dma((peers,)), dma((peers,)),
        ],
        compiler_params=pltpu.CompilerParams(
            collective_id=0, has_side_effects=True, vmem_limit_bytes=56 * 1024 * 1024
        ),
    )(layer_inputs, w_t, w_b, result_sensitivity, rate, events)
    whole = pl.BlockSpec(memory_space=pl.ANY)
    input_t, weight_t = pl.pallas_call(
        write,
        out_shape=(
            jax.ShapeDtypeStruct((rows, iblk), BF16),
            jax.ShapeDtypeStruct((3 * DH, blk), BF16),
        ),
        in_specs=[vmem] * 3,
        out_specs=(whole, whole),
        scratch_shapes=[
            pltpu.VMEM((3 * DH, blk), BF16),
            dma((WRITE_CHUNKS + 1,)),
        ],
        compiler_params=pltpu.CompilerParams(vmem_limit_bytes=16 * 1024 * 1024),
    )(input_sum, summed, factor)
    weight_grad = weight_t.reshape(3, DH, blk).transpose(2, 0, 1)
    return input_t.T, weight_grad


def solution(mesh):
    return jax.shard_map(
        functools.partial(body, mesh.shape["seq"], mesh.shape["tensor"]),
        mesh=mesh,
        in_specs=(P("seq", None), P(None, None, "tensor"), P("seq", "tensor"), P("tensor"), P()),
        out_specs=(P("tensor", "seq"), P("seq", None, "tensor")),
        check_vma=False,
    )
```
